512 devices in a mesh: outer: 32 (over z_lo, y, core), inner: 16 (over x, z_hi).
Axes of the slice: x: 4, y: 8, z: 8 (z_hi: 4, z_lo: 2; z = z_hi * 2 + z_lo), core: 2. Of those that a mesh axis runs over, the one named last changes fastest.
Arguments:
- inputs: bfloat16 [65536, 8192], P(('outer', 'inner')), may hold values from -6 to 6
- segment_ids: int32 [512, 128], P(('outer', 'inner')), may hold values from 0 to 7, never falling along the last dimension, each value on 1 to 32 neighbouring positions
- qkv_weight: bfloat16 [8192, 768], P('inner'), may hold values from -0.0625 to 0.0625
- attn_cotangent: bfloat16 [65536, 512], P(('outer', 'inner')), may hold values from -6 to 6
Outputs:
- input_grad: bfloat16 [65536, 8192], P(('outer', 'inner'))
- weight_grad: float32 [8192, 768], P('inner', 'outer')
The draws below stay inside these ranges and needn't reach their ends.
Inputs may be any that keep to these rules, and one draw needn't show every extreme that they name: `segment_ids`: within each sequence the ids never fall, and each id covers one run of 1 to 32 tokens.
All inputs are finite; a program needn't handle non-finite values.
Results may differ from the reference program's by a relative error of at most 0.033.
Values may be sent and summed in bfloat16 or wider, within the bound.
No kernel may reach another device: no remote copies, remote signals or barrier semaphores. Data moves between devices by JAX's collectives and lax.ppermute only.
A program may use at most 64 MiB of HBM per device.

```python
import math
import jax
import jax.numpy as jnp
import numpy as np
from jax import lax

D = 8192
HD = 128
QH = 4
SEQ = 128
COLS = 768
SEQS = 512
TOKENS = 65536
N_OUTER = 32
N_INNER = 16


def level_of(own_key, shape, pieces, low, top_value):
    gain = 1.0
    for position, parts in pieces:
        steps = jax.random.uniform(jax.random.fold_in(jax.random.fold_in(own_key, 6), position), (parts,), jnp.float32, low / len(pieces), top_value / len(pieces))
        gain = gain * jnp.repeat(jnp.exp(steps), shape[position] // parts).reshape((-1,) + (1,) * (len(shape) - 1 - position))
    return gain


def split_up(count, total, reach, lean):
    portions = [(1 << 20) // math.isqrt(standing ** lean) + 1 for standing in range(2, count + 1)]
    surplus, given = total - reach - (count - 1), [1] * (count - 1)
    while surplus > 0:
        movable = [i for i in range(count - 1) if given[i] < reach]
        whole, budget = sum([portions[i] for i in movable]), surplus
        for i in movable:
            extra = min(reach - given[i], max(1, budget * portions[i] // whole), surplus)
            given[i] = given[i] + extra
            surplus = surplus - extra
    return np.array([reach] + given)


def ragged(own_key, amount, total, bound, slope):
    if amount == 2:
        one = jax.random.randint(own_key, (), max(1, total - bound), min(bound, total - 1) + 1)
        return jnp.stack([one, total - one])
    sizes = jnp.asarray(split_up(amount, total, bound, slope), jnp.int32)
    twos = (amount - 1) // 2
    giver, taker = sizes[1:1 + 2 * twos:2], sizes[2:2 + 2 * twos:2]
    room = jnp.minimum(giver - 1, bound - taker)
    passed = jax.random.randint(jax.random.fold_in(own_key, 1), (twos,), 0, 1 << 20) % (room + 1)
    sizes = sizes.at[1:1 + 2 * twos:2].set(giver - passed).at[2:2 + 2 * twos:2].set(taker + passed)
    return sizes[jax.random.permutation(jax.random.fold_in(own_key, 2), amount)]


def scatter_about(own_key, dims, spread, bound, shards=(), dtype=jnp.bfloat16):
    gain = level_of(own_key, dims, shards, -0.22, 0.18) if shards else 1.0
    result = jax.random.normal(own_key, dims, jnp.float32) * spread * gain
    return jnp.minimum(jnp.maximum(result, -bound), bound).astype(dtype)


def setup_inputs(seed: int = 0) -> dict:
    key_of = jax.random.split(jax.random.key(seed), 5)
    inputs = scatter_about(key_of[0], (TOKENS, D), 1.0, 6.0, ((0, 512),))
    segment_ids = jax.vmap(lambda own: jnp.searchsorted(jnp.cumsum(ragged(own, 8, SEQ, SEQ // 4, 1)), jnp.arange(SEQ), side="right"))(jax.random.split(key_of[1], SEQS)).reshape((SEQS, SEQ)).astype(jnp.int32)
    qkv_weight = scatter_about(key_of[2], (D, COLS), D ** -0.5, 0.0625, ((0, 16),))
    attn_cotangent = scatter_about(key_of[3], (TOKENS, QH * HD), 1.0, 6.0, ((0, 512),))
    return dict(inputs=inputs, segment_ids=segment_ids, qkv_weight=qkv_weight, attn_cotangent=attn_cotangent)


def attention_grad(projected, cotangent, segments):
    count = projected.shape[0]
    heads = cotangent.shape[1] // HD
    values = projected.astype(jnp.float32)
    query = values[:, :heads * HD].reshape(count, heads, HD)
    keys = values[:, heads * HD:(heads + 1) * HD]
    vals = values[:, (heads + 1) * HD:]
    positions = jnp.arange(count)
    allowed = (positions[:, None] >= positions[None, :]) & (segments[:, None] == segments[None, :])

    def forward(query, keys, vals):
        scores = jnp.einsum('shd,td->hst', query, keys) / math.sqrt(HD)
        scores = jnp.where(allowed[None], scores, 0.0)
        weights = jnp.where(allowed[None], jnp.exp(scores), 0.0)
        weights = weights / lax.optimization_barrier(jnp.sum(weights, axis=2, keepdims=True))
        return jnp.einsum('hst,td->shd', weights, vals).reshape(count, heads * HD)
    unused, pullback = jax.vjp(forward, query, keys, vals)
    grad_q, grad_k, grad_v = pullback(cotangent.astype(jnp.float32))
    return jnp.concatenate([grad_q.reshape(count, heads * HD), grad_k, grad_v], axis=1).astype(jnp.bfloat16)

def reference(inputs, segment_ids, qkv_weight, attn_cotangent):
    per_group = N_INNER * SEQ
    block_width = D // N_INNER
    weight_blocks = qkv_weight.reshape(N_INNER, block_width, COLS)

    def one_group(packed):
        block_x, block_seg, block_cot = packed
        x_blocks = jnp.transpose(block_x.reshape(per_group, N_INNER, block_width), (1, 0, 2))

        def add_block(total, pair):
            part = jnp.dot(pair[0], pair[1], preferred_element_type=jnp.float32).astype(jnp.bfloat16)
            part = lax.optimization_barrier(part)
            return (total + part.astype(jnp.float32), None)
        summed, unused = lax.scan(add_block, jnp.zeros((per_group, COLS), jnp.float32), (x_blocks, weight_blocks))
        projected = summed.astype(jnp.bfloat16)
        grads = jax.vmap(attention_grad)(projected.reshape(N_INNER, SEQ, COLS), block_cot.reshape(N_INNER, SEQ, QH * HD), block_seg)
        grads = grads.reshape(per_group, COLS)
        input_part = jnp.dot(grads, qkv_weight.T, preferred_element_type=jnp.float32).astype(jnp.bfloat16)
        weight_part = jnp.dot(block_x.T, grads, preferred_element_type=jnp.float32).astype(jnp.bfloat16)
        return (input_part, weight_part)
    input_grad, group_grad = lax.map(one_group, (inputs.reshape(N_OUTER, per_group, D), segment_ids.reshape(N_OUTER, N_INNER, SEQ), attn_cotangent.reshape(N_OUTER, per_group, QH * HD)))
    weight_grad = lax.optimization_barrier(jnp.sum(group_grad.astype(jnp.float32), axis=0))
    return (input_grad.reshape(TOKENS, D), weight_grad)
```

```python
import math

import jax
import jax.numpy as jnp
from jax import lax
from jax.experimental import pallas as pl
from jax.experimental.pallas import tpu as pltpu
from jax.sharding import Mesh
from jax.sharding import PartitionSpec as P

HD = 128
BF16 = jnp.bfloat16
F32 = jnp.float32
ANY = pl.BlockSpec(memory_space=pl.ANY)
PARAMS = pltpu.CompilerParams(vmem_limit_bytes=40 * 1024 * 1024)

NT = (((1,), (1,)), ((), ()))
TN = (((0,), (0,)), ((), ()))


def arr(shape, dtype=BF16):
    return jax.ShapeDtypeStruct(shape, dtype)


def cost(flops, nbytes):
    return pl.CostEstimate(flops=flops, bytes_accessed=nbytes, transcendentals=0)


def dot(a, b, dims=(((1,), (0,)), ((), ()))):
    return lax.dot_general(a, b, dims, preferred_element_type=F32)


def split_kernel(x_ref, *rest):
    outs, sems = rest[:-1], rest[-1]
    n = len(outs)
    width = outs[0].shape[1]
    me = lax.axis_index("x")
    copies = []
    for k in range(n):
        start = pl.multiple_of(lax.rem(me + k, n) * width, width)
        copies.append(pltpu.make_async_copy(x_ref.at[:, pl.ds(start, width)], outs[k], sems.at[k]))
    for copy in copies:
        copy.start()
    for copy in copies:
        copy.wait()


def join_kernel(*refs):
    ins, out, sems = refs[:-2], refs[-2], refs[-1]
    n = len(ins)
    width = ins[0].shape[1]
    me = lax.axis_index("x")
    copies = []
    for k in range(n):
        start = pl.multiple_of(lax.rem(me + k, n) * width, width)
        copies.append(pltpu.make_async_copy(ins[k], out.at[:, pl.ds(start, width)], sems.at[k]))
    for copy in copies:
        copy.start()
    for copy in copies:
        copy.wait()


def piece_places(rows):
    zl, zh, c = lax.axis_index("zl"), lax.axis_index("zh"), lax.axis_index("c")
    near = lax.rem(zh + 3 + 2 * zl, 4)
    far = lax.rem(zh + 5 - 2 * zl, 4)
    opposite = lax.rem(zh + 2, 4)
    places = [zh * (2 * rows)]
    for block in (near, far, opposite):
        places.append(block * (2 * rows) + c * rows)
        places.append(block * (2 * rows) + (1 - c) * rows)
    return [pl.multiple_of(p, rows) for p in places]


def forward_kernel(x0, x1, x2, x3, w0, a, a2, b, b2, d, d2, p0, p1, p2, p3, acc):
    rows = a.shape[0]
    places = piece_places(rows)
    xs = (x0, x1, x2, x3)
    tokens = x0.shape[0]
    for i, (place, w) in enumerate(zip(places, (w0, a, a2, b, b2, d, d2))):
        depth = w.shape[0]
        x = jnp.concatenate([r[:, pl.ds(place, depth)] for r in xs], axis=0)
        term = dot(x, w[...])
        if i == 0:
            acc[...] = term
        else:
            acc[...] += term
    for k, p in enumerate((p0, p1, p2, p3)):
        p[...] = acc[k * tokens : (k + 1) * tokens, :].astype(BF16)


def attention_kernel(p0, p1, p2, p3, seg_ref, cot_ref, out):
    total = p0[...].astype(F32) + p1[...].astype(F32) + p2[...].astype(F32) + p3[...].astype(F32)
    projected = total.astype(BF16)
    count = projected.shape[0]
    heads = cot_ref.shape[1] // HD
    row = jnp.broadcast_to(seg_ref[...], (count, count))
    col = row.T
    here = lax.broadcasted_iota(jnp.int32, (count, count), 0)
    there = lax.broadcasted_iota(jnp.int32, (count, count), 1)
    allowed = (here >= there) & (row == col)
    keys = projected[:, heads * HD : (heads + 1) * HD]
    vals = projected[:, (heads + 1) * HD :]
    scale = 1.0 / math.sqrt(HD)
    grad_k = jnp.zeros((count, HD), F32)
    grad_v = jnp.zeros((count, HD), F32)
    for h in range(heads):
        query = projected[:, h * HD : (h + 1) * HD]
        cot = cot_ref[:, h * HD : (h + 1) * HD]
        scores = dot(query, keys, NT) * scale
        scores = jnp.where(allowed, scores, 0.0)
        weights = jnp.where(allowed, jnp.exp(scores), 0.0)
        weights = weights / jnp.sum(weights, axis=1, keepdims=True)
        grad_w = dot(cot, vals, NT)
        lean = jnp.sum(weights * grad_w, axis=1, keepdims=True)
        grad_s = (weights * (grad_w - lean) * scale).astype(BF16)
        out[:, h * HD : (h + 1) * HD] = dot(grad_s, keys).astype(BF16)
        grad_k += dot(grad_s, query, TN)
        grad_v += dot(weights.astype(BF16), cot, TN)
    out[:, heads * HD : (heads + 1) * HD] = grad_k.astype(BF16)
    out[:, (heads + 1) * HD :] = grad_v.astype(BF16)


def weight_kernel(g0, g1, g2, g3, x0, x1, x2, x3, mine, other):
    groups, span, wide = mine.shape
    zl, y, c = lax.axis_index("zl"), lax.axis_index("y"), lax.axis_index("c")
    zh = lax.axis_index("zh")
    grads = jnp.concatenate([g0[...], g1[...], g2[...], g3[...]], axis=0)
    cols = grads.shape[1]
    n_y = groups // 2
    shape = (groups * span, cols)
    place = lax.broadcasted_iota(jnp.int32, shape, 0)
    source = lax.broadcasted_iota(jnp.int32, shape, 1)
    group, within = place // span, place % span
    at_z = lax.rem(zl + group // n_y, 2)
    at_y = lax.rem(y + group % n_y, n_y)
    left = []
    for core in (c, 1 - c):
        wanted = ((at_z * n_y + at_y) * 2 + core) * span + within
        pick = jnp.where(source == wanted, 1.0, 0.0).astype(BF16)
        left.append(dot(pick, grads, NT).astype(BF16))
    tile = 256
    block = wide // 4
    for kz in range(4):
        for t in range(block // tile):
            start = pl.multiple_of(lax.rem(zh + kz, 4) * block + t * tile, tile)
            x = jnp.concatenate([r[:, pl.ds(start, tile)] for r in (x0, x1, x2, x3)], axis=0)
            at = kz * block + t * tile
            other[:, :, at : at + tile] = dot(left[1], x).astype(BF16).reshape(groups, span, tile)
            mine[:, :, at : at + tile] = dot(left[0], x).reshape(groups, span, tile)


def input_kernel(g0, g1, g2, g3, w0, a, a2, b, b2, d, d2, o0, o1, o2, o3):
    rows = a.shape[0]
    tokens = g0.shape[0]
    places = piece_places(rows)
    grads = jnp.concatenate([g0[...], g1[...], g2[...], g3[...]], axis=0)
    for place, w in zip(places, (w0, a, a2, b, b2, d, d2)):
        depth = w.shape[0]
        term = dot(grads, w[...], NT).astype(BF16)
        for k, o in enumerate((o0, o1, o2, o3)):
            o[:, pl.ds(place, depth)] = term[k * tokens : (k + 1) * tokens]


def first_kernel(mine, got, *outs):
    groups, span, wide = mine.shape
    n_y = groups // 2
    block = wide // 4
    half = block // 2
    for lz in range(2):
        for ky in range(n_y):
            g = lz * n_y + ky
            total = mine[g] + got[g].astype(F32)
            for kz in range(4):
                at = kz * block
                outs[ky][lz, :, kz * half : (kz + 1) * half] = total[:, at : at + half].astype(BF16)
                outs[n_y + lz * 4 + kz][ky] = total[:, at + half : at + block].astype(BF16)


def second_kernel(*refs):
    ins, outs = refs[:16], refs[16:]
    half = ins[8].shape[2]
    first = sum(r[...].astype(F32) for r in ins[:8])
    second = sum(r[...].astype(F32) for r in ins[8:])
    for lz in range(2):
        for kz in range(4):
            outs[lz * 4 + kz][...] = first[lz, :, kz * half : (kz + 1) * half].astype(BF16)
    for ky in range(8):
        outs[8 + ky][...] = second[ky].astype(BF16)


def third_kernel(*refs):
    ins, out = refs[:16], refs[16]
    half = ins[0].shape[1]
    out[:, :half] = sum(r[...].astype(F32) for r in ins[:8])
    out[:, half:] = sum(r[...].astype(F32) for r in ins[8:])


def shift(value, axis, k):
    n = lax.axis_size(axis)
    return lax.ppermute(value, axis, [(i, (i + k) % n) for i in range(n)])


def z_move(value, target):
    pairs = []
    for zl in range(2):
        for zh in range(4):
            to_l, to_h = target(zl, zh)
            pairs.append((zl * 4 + zh, to_l * 4 + to_h % 4))
    return lax.ppermute(value, ("zl", "zh"), pairs)


def across(value):
    return z_move(value, lambda zl, zh: (0, zh + 1) if zl else (1, zh - 1))


def beside(value):
    return z_move(value, lambda zl, zh: (1 - zl, zh))


def on_device(inputs, segment_ids, qkv_weight, attn_cotangent):
    tokens, features = inputs.shape
    block, cols = qkv_weight.shape
    n = 4
    width = features // n
    half = block // 2
    n_y = 8
    span = cols // 32
    c = lax.axis_index("c")

    sent = pl.pallas_call(
        split_kernel,
        out_shape=[arr((tokens, width))] * n,
        in_specs=[ANY],
        out_specs=[ANY] * n,
        scratch_shapes=[pltpu.SemaphoreType.DMA((n,))],
        name="split_features",
    )(inputs)
    own = lax.dynamic_slice_in_dim(qkv_weight, c * half, half, 0)
    a = across(own)
    x2 = shift(sent[2], "x", 2)
    x1 = shift(sent[1], "x", 1)
    x3 = shift(sent[3], "x", 3)
    a2 = shift(a, "c", 1)
    b = beside(a)
    b2 = shift(b, "c", 1)
    d = across(b)
    d2 = shift(d, "c", 1)
    xs = (sent[0], x1, x2, x3)
    weights = (qkv_weight, a, a2, b, b2, d, d2)

    flops = 2 * n * tokens * width * cols
    parts = pl.pallas_call(
        forward_kernel,
        out_shape=[arr((tokens, cols))] * n,
        scratch_shapes=[pltpu.VMEM((n * tokens, cols), F32)],
        compiler_params=PARAMS,
        cost_estimate=cost(flops, 6 << 20),
        name="forward",
    )(*xs, *weights)
    back = [parts[0]] + [shift(parts[k], "x", n - k) for k in range(1, n)]

    grads = pl.pallas_call(
        attention_kernel,
        out_shape=arr((tokens, cols)),
        compiler_params=PARAMS,
        cost_estimate=cost(1 << 28, 1 << 20),
        name="attention",
    )(*back, segment_ids, attn_cotangent)
    gs = [grads] + [shift(grads, "x", k) for k in range(1, n)]

    mine, other = pl.pallas_call(
        weight_kernel,
        out_shape=[arr((2 * n_y, span, width), F32), arr((2 * n_y, span, width))],
        compiler_params=PARAMS,
        cost_estimate=cost(flops, 8 << 20),
        name="weight_grad",
    )(*gs, *xs)
    got = shift(other, "c", 1)

    back = pl.pallas_call(
        input_kernel,
        out_shape=[arr((tokens, width))] * n,
        compiler_params=PARAMS,
        cost_estimate=cost(flops, 6 << 20),
        name="input_grad",
    )(*gs, *weights)
    home = [back[0]] + [shift(back[k], "x", n - k) for k in range(1, n)]

    pieces = pl.pallas_call(
        first_kernel,
        out_shape=[arr((2, span, n * half))] * n_y + [arr((n_y, span, half))] * 8,
        compiler_params=PARAMS,
        cost_estimate=cost(1 << 20, 8 << 20),
        name="add_cores",
    )(mine, got)

    def spread_y(values):
        return [values[0]] + [shift(values[k], "y", k) for k in range(1, n_y)]

    def spread_z(values):
        out = [values[0]]
        for i in range(1, 8):
            lz, kz = divmod(i, 4)
            out.append(z_move(values[i], lambda zl, zh: ((zl + lz) % 2, zh + kz)))
        return out

    pieces = spread_y(pieces[:8]) + spread_z(pieces[8:])
    pieces = pl.pallas_call(
        second_kernel,
        out_shape=[arr((span, half))] * 16,
        compiler_params=PARAMS,
        cost_estimate=cost(1 << 20, 2 << 20),
        name="add_first",
    )(*pieces)
    pieces = spread_z(pieces[:8]) + spread_y(pieces[8:])
    weight_grad = pl.pallas_call(
        third_kernel,
        out_shape=arr((span, block), F32),
        compiler_params=PARAMS,
        cost_estimate=cost(1 << 18, 1 << 18),
        name="add_second",
    )(*pieces).T

    input_grad = pl.pallas_call(
        join_kernel,
        out_shape=arr((tokens, features)),
        in_specs=[ANY] * n,
        out_specs=ANY,
        scratch_shapes=[pltpu.SemaphoreType.DMA((n,))],
        name="join_features",
    )(*home)
    return (input_grad, weight_grad)


def solution(mesh):
    outer, inner = ("zl", "y", "c"), ("x", "zh")
    fine = Mesh(mesh.devices.reshape(2, 8, 2, 4, 4), outer + inner)
    return jax.shard_map(
        on_device,
        mesh=fine,
        in_specs=(
            P(outer + inner, None),
            P(outer + inner, None),
            P(inner, None),
            P(outer + inner, None),
        ),
        out_specs=(P(outer + inner, None), P(inner, outer)),
        check_vma=False,
    )
```

```python
import math

import jax
import jax.numpy as jnp
from jax import lax
from jax.experimental import pallas as pl
from jax.experimental.pallas import tpu as pltpu
from jax.sharding import Mesh
from jax.sharding import PartitionSpec as P

HD = 128
BF16 = jnp.bfloat16
F32 = jnp.float32
PARAMS = pltpu.CompilerParams(vmem_limit_bytes=40 * 1024 * 1024)

NT = (((1,), (1,)), ((), ()))
TN = (((0,), (0,)), ((), ()))


def arr(shape, dtype=BF16):
    return jax.ShapeDtypeStruct(shape, dtype)


def cost(flops, nbytes):
    return pl.CostEstimate(flops=flops, bytes_accessed=nbytes, transcendentals=0)


def dot(a, b, dims=(((1,), (0,)), ((), ()))):
    return lax.dot_general(a, b, dims, preferred_element_type=F32)


def join_kernel(*refs):
    ins, out = refs[:-1], refs[-1]
    n = len(ins)
    width = ins[0].shape[1]
    me = lax.axis_index("x")
    for k in range(n):
        start = pl.multiple_of(lax.rem(me + k, n) * width, width)
        out[:, pl.ds(start, width)] = ins[k][...]


def piece_places(rows):
    zl, zh, c = lax.axis_index("zl"), lax.axis_index("zh"), lax.axis_index("c")
    near = lax.rem(zh + 3 + 2 * zl, 4)
    far = lax.rem(zh + 5 - 2 * zl, 4)
    opposite = lax.rem(zh + 2, 4)
    places = [zh * (2 * rows)]
    for block in (near, far, opposite):
        places.append(block * (2 * rows) + c * rows)
        places.append(block * (2 * rows) + (1 - c) * rows)
    return [pl.multiple_of(p, rows) for p in places]


def forward_kernel(x0, x1, x2, x3, w0, a, a2, b, b2, d, d2, parts, acc):
    rows = a.shape[0]
    places = piece_places(rows)
    xs = (x0, x1, x2, x3)
    tokens = x0.shape[0]
    for i, (place, w) in enumerate(zip(places, (w0, a, a2, b, b2, d, d2))):
        depth = w.shape[0]
        x = jnp.concatenate([r[:, pl.ds(place, depth)] for r in xs], axis=0)
        term = dot(x, w[...])
        if i == 0:
            acc[...] = term
        else:
            acc[...] += term
    me = lax.axis_index("x")
    for k in range(4):
        parts[lax.rem(me + 4 - k, 4)] = acc[k * tokens : (k + 1) * tokens, :].astype(BF16)


def attention_kernel(parts, seg_ref, cot_ref, out):
    total = sum(parts[k].astype(F32) for k in range(4))
    projected = total.astype(BF16)
    count = projected.shape[0]
    heads = cot_ref.shape[1] // HD
    row = jnp.broadcast_to(seg_ref[...], (count, count))
    col = row.T
    here = lax.broadcasted_iota(jnp.int32, (count, count), 0)
    there = lax.broadcasted_iota(jnp.int32, (count, count), 1)
    allowed = (here >= there) & (row == col)
    keys = projected[:, heads * HD : (heads + 1) * HD]
    vals = projected[:, (heads + 1) * HD :]
    scale = 1.0 / math.sqrt(HD)
    grad_k = jnp.zeros((count, HD), F32)
    grad_v = jnp.zeros((count, HD), F32)
    for h in range(heads):
        query = projected[:, h * HD : (h + 1) * HD]
        cot = cot_ref[:, h * HD : (h + 1) * HD]
        scores = dot(query, keys, NT) * scale
        scores = jnp.where(allowed, scores, 0.0)
        weights = jnp.where(allowed, jnp.exp(scores), 0.0)
        weights = weights / jnp.sum(weights, axis=1, keepdims=True)
        grad_w = dot(cot, vals, NT)
        lean = jnp.sum(weights * grad_w, axis=1, keepdims=True)
        grad_s = (weights * (grad_w - lean) * scale).astype(BF16)
        out[:, h * HD : (h + 1) * HD] = dot(grad_s, keys).astype(BF16)
        grad_k += dot(grad_s, query, TN)
        grad_v += dot(weights.astype(BF16), cot, TN)
    out[:, heads * HD : (heads + 1) * HD] = grad_k.astype(BF16)
    out[:, (heads + 1) * HD :] = grad_v.astype(BF16)


def relative(gathered):
    me = lax.axis_index("x")
    return jnp.concatenate([gathered[lax.rem(me + 4 - k, 4)] for k in range(4)], axis=0)


def weight_kernel(g, x0, x1, x2, x3, mine, other):
    pieces, span, block = mine.shape
    groups = pieces // 4
    c = lax.axis_index("c")
    grads = relative(g)
    shape = (groups * span, grads.shape[1])
    place = lax.broadcasted_iota(jnp.int32, shape, 0)
    source = lax.broadcasted_iota(jnp.int32, shape, 1)
    left = []
    for core in (c, 1 - c):
        wanted = (place // span * 2 + core) * span + place % span
        pick = jnp.where(source == wanted, 1.0, 0.0).astype(BF16)
        left.append(dot(pick, grads, NT).astype(BF16))
    tile = 256
    for zh in range(4):
        for at in range(0, block, tile):
            start = zh * block + at
            x = jnp.concatenate([r[:, start : start + tile] for r in (x0, x1, x2, x3)], axis=0)
            for out, rows in ((other, left[1]), (mine, left[0])):
                term = dot(rows, x)
                for k in range(groups):
                    out[k * 4 + zh, :, at : at + tile] = term[k * span : (k + 1) * span].astype(out.dtype)


def input_kernel(g, w0, a, a2, b, b2, d, d2, o0, o1, o2, o3):
    rows = a.shape[0]
    tokens = g.shape[1]
    places = piece_places(rows)
    grads = relative(g)
    for place, w in zip(places, (w0, a, a2, b, b2, d, d2)):
        depth = w.shape[0]
        term = dot(grads, w[...], NT).astype(BF16)
        for k, o in enumerate((o0, o1, o2, o3)):
            o[:, pl.ds(place, depth)] = term[k * tokens : (k + 1) * tokens]


def add_kernel(mine, got, out):
    out[...] = (mine[...] + got[...].astype(F32)).astype(BF16)


def total_kernel(ref, out):
    out[...] = jnp.sum(ref[...].astype(F32), axis=0)


def shift(value, axis, k):
    n = lax.axis_size(axis)
    return lax.ppermute(value, axis, [(i, (i + k) % n) for i in range(n)])


def z_move(value, target):
    pairs = []
    for zl in range(2):
        for zh in range(4):
            to_l, to_h = target(zl, zh)
            pairs.append((zl * 4 + zh, to_l * 4 + to_h % 4))
    return lax.ppermute(value, ("zl", "zh"), pairs)


def across(value):
    return z_move(value, lambda zl, zh: (0, zh + 1) if zl else (1, zh - 1))


def beside(value):
    return z_move(value, lambda zl, zh: (1 - zl, zh))


def on_device(inputs, segment_ids, qkv_weight, attn_cotangent):
    tokens, features = inputs.shape
    block, cols = qkv_weight.shape
    n = 4
    width = features // n
    half = block // 2
    span = cols // 32
    c = lax.axis_index("c")

    me = lax.axis_index("x")
    sent = [lax.dynamic_slice_in_dim(inputs, lax.rem(me + k, n) * width, width, 1) for k in range(n)]
    own = lax.dynamic_slice_in_dim(qkv_weight, c * half, half, 0)
    a = across(own)
    x2 = shift(sent[2], "x", 2)
    x1 = shift(sent[1], "x", 1)
    x3 = shift(sent[3], "x", 3)
    a2 = shift(a, "c", 1)
    b = beside(a)
    b2 = shift(b, "c", 1)
    d = across(b)
    d2 = shift(d, "c", 1)
    xs = (sent[0], x1, x2, x3)
    weights = (qkv_weight, a, a2, b, b2, d, d2)

    flops = 2 * n * tokens * width * cols
    parts = pl.pallas_call(
        forward_kernel,
        out_shape=arr((n, tokens, cols)),
        scratch_shapes=[pltpu.VMEM((n * tokens, cols), F32)],
        compiler_params=PARAMS,
        cost_estimate=cost(flops, 6 << 20),
        name="forward",
    )(*xs, *weights)
    parts = lax.all_to_all(parts, "x", 0, 0, tiled=True)

    grads = pl.pallas_call(
        attention_kernel,
        out_shape=arr((tokens, cols)),
        compiler_params=PARAMS,
        cost_estimate=cost(1 << 28, 1 << 20),
        name="attention",
    )(parts, segment_ids, attn_cotangent)
    grads = lax.all_gather(grads, "x", axis=0, tiled=False)

    mine, other = pl.pallas_call(
        weight_kernel,
        out_shape=[arr((64, span, block), F32), arr((64, span, block))],
        compiler_params=PARAMS,
        cost_estimate=cost(flops, 8 << 20),
        name="weight_grad",
    )(grads, *xs)
    got = shift(other, "c", 1)

    back = pl.pallas_call(
        input_kernel,
        out_shape=[arr((tokens, width))] * n,
        compiler_params=PARAMS,
        cost_estimate=cost(flops, 6 << 20),
        name="input_grad",
    )(grads, *weights)
    home = [back[0]] + [shift(back[k], "x", n - k) for k in (2, 1, 3)]

    summed = pl.pallas_call(
        add_kernel,
        out_shape=arr((64, span, block)),
        compiler_params=PARAMS,
        cost_estimate=cost(1 << 20, 8 << 20),
        name="add_cores",
    )(mine, got)
    pieces = lax.all_to_all(summed, ("zl", "y", "zh"), 0, 0, tiled=True)
    weight_grad = pl.pallas_call(
        total_kernel,
        out_shape=arr((span, block), F32),
        compiler_params=PARAMS,
        cost_estimate=cost(1 << 20, 2 << 20),
        name="add_replicas",
    )(pieces).T

    input_grad = pl.pallas_call(
        join_kernel,
        out_shape=arr((tokens, features)),
        compiler_params=PARAMS,
        cost_estimate=cost(1 << 20, 4 << 20),
        name="join_features",
    )(home[0], home[2], home[1], home[3])
    return (input_grad, weight_grad)


def solution(mesh):
    outer, inner = ("zl", "y", "c"), ("x", "zh")
    fine = Mesh(mesh.devices.reshape(2, 8, 2, 4, 4), outer + inner)
    return jax.shard_map(
        on_device,
        mesh=fine,
        in_specs=(
            P(outer + inner, None),
            P(outer + inner, None),
            P(inner, None),
            P(outer + inner, None),
        ),
        out_specs=(P(outer + inner, None), P(inner, outer)),
        check_vma=False,
    )
```

```python
import math

import jax
import jax.numpy as jnp
from jax import lax
from jax.experimental import pallas as pl
from jax.experimental.pallas import tpu as pltpu
from jax.sharding import Mesh
from jax.sharding import PartitionSpec as P

HD = 128
BF16 = jnp.bfloat16
F32 = jnp.float32
PARAMS = pltpu.CompilerParams(vmem_limit_bytes=20 * 1024 * 1024)

NT = (((1,), (1,)), ((), ()))
TN = (((0,), (0,)), ((), ()))


def arr(shape, dtype=BF16):
    return jax.ShapeDtypeStruct(shape, dtype)


def cost(flops, nbytes):
    return pl.CostEstimate(flops=flops, bytes_accessed=nbytes, transcendentals=0)


def dot(a, b, dims=(((1,), (0,)), ((), ()))):
    return lax.dot_general(a, b, dims, preferred_element_type=F32)


def join_kernel(*refs):
    ins, out = refs[:-1], refs[-1]
    n = len(ins)
    width = ins[0].shape[1]
    me = lax.axis_index("x")
    for k in range(n):
        start = pl.multiple_of(lax.rem(me + k, n) * width, width)
        out[:, pl.ds(start, width)] = ins[k][...]


def piece_places(rows):
    zl, zh, c = lax.axis_index("zl"), lax.axis_index("zh"), lax.axis_index("c")
    near = lax.rem(zh + 3 + 2 * zl, 4)
    far = lax.rem(zh + 5 - 2 * zl, 4)
    opposite = lax.rem(zh + 2, 4)
    places = [zh * (2 * rows)]
    for block in (near, far, opposite):
        places.append(block * (2 * rows) + c * rows)
        places.append(block * (2 * rows) + (1 - c) * rows)
    return [pl.multiple_of(p, rows) for p in places]


def forward_kernel(x0, x1, x2, x3, w0, a, a2, b, b2, d, d2, parts, whole, acc):
    rows = a.shape[0]
    tokens = x0.shape[0]
    me = lax.axis_index("x")
    for i, (place, w) in enumerate(zip(piece_places(rows), (w0, a, a2, b, b2, d, d2))):
        depth = w.shape[0]
        x = jnp.concatenate([r[:, pl.ds(place, depth)] for r in (x0, x1, x2, x3)], axis=0)
        whole[pl.ds(place, depth), :] = w[...]
        term = dot(x, w[...])
        if i == 0:
            acc[...] = term
        else:
            acc[...] += term
    for k in range(4):
        parts[lax.rem(me + 4 - k, 4)] = acc[k * tokens : (k + 1) * tokens, :].astype(BF16)


def attention_kernel(parts, seg_ref, cot_ref, out):
    total = sum(parts[k].astype(F32) for k in range(4))
    projected = total.astype(BF16)
    count = projected.shape[0]
    heads = cot_ref.shape[1] // HD
    row = jnp.broadcast_to(seg_ref[...], (count, count))
    col = row.T
    here = lax.broadcasted_iota(jnp.int32, (count, count), 0)
    there = lax.broadcasted_iota(jnp.int32, (count, count), 1)
    allowed = (here >= there) & (row == col)
    keys = projected[:, heads * HD : (heads + 1) * HD]
    vals = projected[:, (heads + 1) * HD :]
    scale = 1.0 / math.sqrt(HD)
    grad_k = jnp.zeros((count, HD), F32)
    grad_v = jnp.zeros((count, HD), F32)
    for h in range(heads):
        query = projected[:, h * HD : (h + 1) * HD]
        cot = cot_ref[:, h * HD : (h + 1) * HD]
        scores = dot(query, keys, NT) * scale
        scores = jnp.where(allowed, scores, 0.0)
        weights = jnp.where(allowed, jnp.exp(scores), 0.0)
        weights = weights / jnp.sum(weights, axis=1, keepdims=True)
        grad_w = dot(cot, vals, NT)
        lean = jnp.sum(weights * grad_w, axis=1, keepdims=True)
        grad_s = (weights * (grad_w - lean) * scale).astype(BF16)
        out[:, h * HD : (h + 1) * HD] = dot(grad_s, keys).astype(BF16)
        grad_k += dot(grad_s, query, TN)
        grad_v += dot(weights.astype(BF16), cot, TN)
    out[:, heads * HD : (heads + 1) * HD] = grad_k.astype(BF16)
    out[:, (heads + 1) * HD :] = grad_v.astype(BF16)


def relative(g):
    n = g.shape[0]
    me = lax.axis_index("x")
    return jnp.concatenate([g[lax.rem(me + n - k, n)] for k in range(n)], axis=0)


def weight_terms(g, xs, core, shape):
    pieces, span, block = shape
    cols = g.shape[2]
    place = lax.broadcasted_iota(jnp.int32, (cols // 2, cols), 0)
    source = lax.broadcasted_iota(jnp.int32, (cols // 2, cols), 1)
    wanted = (place // span * 2 + core) * span + place % span
    pick = jnp.where(source == wanted, 1.0, 0.0).astype(BF16)
    left = dot(pick, relative(g), NT).astype(BF16)
    tile = 256
    for zh in range(4):
        for at in range(0, block, tile):
            start = zh * block + at
            term = dot(left, jnp.concatenate([r[:, start : start + tile] for r in xs], axis=0))
            for k in range(pieces // 4):
                yield (k * 4 + zh, slice(None), slice(at, at + tile)), term[k * span : (k + 1) * span]


def other_kernel(g, x0, x1, x2, x3, out):
    for at, piece in weight_terms(g, (x0, x1, x2, x3), 1 - lax.axis_index("c"), out.shape):
        out[at] = piece.astype(BF16)


def mine_kernel(g, x0, x1, x2, x3, got, out):
    for at, piece in weight_terms(g, (x0, x1, x2, x3), lax.axis_index("c"), out.shape):
        out[at] = (piece + got[at].astype(F32)).astype(BF16)


def input_kernel(g, whole, *outs):
    n, tokens, _ = g.shape
    grads = relative(g)
    tile = 256
    for at in range(0, whole.shape[0], tile):
        term = dot(grads, whole[at : at + tile, :], NT).astype(BF16)
        for k, out in enumerate(outs):
            out[:, at : at + tile] = term[k * tokens : (k + 1) * tokens]


def total_kernel(ref, out):
    out[...] = jnp.sum(ref[...].astype(F32), axis=0)


def shift(value, axis, k):
    n = lax.axis_size(axis)
    return lax.ppermute(value, axis, [(i, (i + k) % n) for i in range(n)])


def swap(value, axes):
    return lax.all_to_all(value, axes, 0, 0, tiled=True)


def z_move(value, target):
    pairs = []
    for zl in range(2):
        for zh in range(4):
            to_l, to_h = target(zl, zh)
            pairs.append((zl * 4 + zh, to_l * 4 + to_h % 4))
    return lax.ppermute(value, ("zl", "zh"), pairs)


def across(value):
    return z_move(value, lambda zl, zh: (0, zh + 1) if zl else (1, zh - 1))


def beside(value):
    return z_move(value, lambda zl, zh: (1 - zl, zh))


def on_device(inputs, segment_ids, qkv_weight, attn_cotangent):
    tokens, features = inputs.shape
    block, cols = qkv_weight.shape
    n = 4
    width = features // n
    half = block // 2
    span = cols // 32
    c = lax.axis_index("c")

    me = lax.axis_index("x")
    sent = [lax.dynamic_slice_in_dim(inputs, lax.rem(me + k, n) * width, width, 1) for k in range(n)]
    own = lax.dynamic_slice_in_dim(qkv_weight, c * half, half, 0)
    a = across(own)
    x1 = shift(sent[1], "x", 1)
    x3 = shift(sent[3], "x", 3)
    x2 = shift(sent[2], "x", 2)
    a2 = shift(a, "c", 1)
    b = beside(a)
    b, x1, x3 = lax.optimization_barrier((b, x1, x3))
    b2 = shift(b, "c", 1)
    d = across(b)
    d2 = shift(d, "c", 1)
    xs = (sent[0], x1, x2, x3)
    weights = (qkv_weight, a, a2, b, b2, d, d2)

    flops = 2 * n * tokens * width * cols
    parts, whole = pl.pallas_call(
        forward_kernel,
        out_shape=[arr((n, tokens, cols)), arr((width, cols))],
        scratch_shapes=[pltpu.VMEM((n * tokens, cols), F32)],
        compiler_params=PARAMS,
        cost_estimate=cost(flops, 6 << 20),
        name="forward",
    )(*xs, *weights)
    parts = swap(parts, "x")

    grads = pl.pallas_call(
        attention_kernel,
        out_shape=arr((tokens, cols)),
        compiler_params=PARAMS,
        cost_estimate=cost(1 << 28, 1 << 20),
        name="attention",
    )(parts, segment_ids, attn_cotangent)
    grads = lax.all_gather(grads, "x", axis=0, tiled=False)

    share = arr((64, span, block))
    other = pl.pallas_call(
        other_kernel,
        out_shape=share,
        compiler_params=PARAMS,
        cost_estimate=cost(flops // 2, 4 << 20),
        name="weight_grad_other_core",
    )(grads, *xs)
    got = shift(other, "c", 1)

    back = pl.pallas_call(
        input_kernel,
        out_shape=[arr((tokens, width))] * n,
        compiler_params=PARAMS,
        cost_estimate=cost(flops, 6 << 20),
        name="input_grad",
    )(grads, whole)
    got, back = lax.optimization_barrier((got, back))
    home = [back[0]] + [shift(back[k], "x", n - k) for k in range(1, n)]

    summed = pl.pallas_call(
        mine_kernel,
        out_shape=share,
        compiler_params=PARAMS,
        cost_estimate=cost(flops // 2, 6 << 20),
        name="weight_grad_this_core",
    )(grads, *xs, got)
    pieces = swap(summed, ("zl", "y", "zh"))
    weight_grad = pl.pallas_call(
        total_kernel,
        out_shape=arr((span, block), F32),
        compiler_params=PARAMS,
        cost_estimate=cost(1 << 20, 2 << 20),
        name="add_replicas",
    )(pieces).T

    input_grad = pl.pallas_call(
        join_kernel,
        out_shape=arr((tokens, features)),
        compiler_params=PARAMS,
        cost_estimate=cost(1 << 20, 4 << 20),
        name="join_features",
    )(*home)
    return (input_grad, weight_grad)


def solution(mesh):
    outer, inner = ("zl", "y", "c"), ("x", "zh")
    fine = Mesh(mesh.devices.reshape(2, 8, 2, 4, 4), outer + inner)
    return jax.shard_map(
        on_device,
        mesh=fine,
        in_specs=(
            P(outer + inner, None),
            P(outer + inner, None),
            P(inner, None),
            P(outer + inner, None),
        ),
        out_specs=(P(outer + inner, None), P(inner, outer)),
        check_vma=False,
    )
```

```python
import math

import jax
import jax.numpy as jnp
from jax import lax
from jax.experimental import pallas as pl
from jax.experimental.pallas import tpu as pltpu
from jax.sharding import Mesh
from jax.sharding import PartitionSpec as P

HD = 128
BF16 = jnp.bfloat16
F32 = jnp.float32
PARAMS = pltpu.CompilerParams(vmem_limit_bytes=20 * 1024 * 1024)

NT = (((1,), (1,)), ((), ()))
TN = (((0,), (0,)), ((), ()))


def arr(shape, dtype=BF16):
    return jax.ShapeDtypeStruct(shape, dtype)


def cost(flops, nbytes):
    return pl.CostEstimate(flops=flops, bytes_accessed=nbytes, transcendentals=0)


def dot(a, b, dims=(((1,), (0,)), ((), ()))):
    return lax.dot_general(a, b, dims, preferred_element_type=F32)


def join_kernel(*refs):
    ins, out = refs[:-1], refs[-1]
    n = len(ins)
    width = ins[0].shape[1]
    me = lax.axis_index("x")
    for k in range(n):
        start = pl.multiple_of(lax.rem(me + k, n) * width, width)
        out[:, pl.ds(start, width)] = ins[k][...]


def piece_places(rows):
    zl, zh, c = lax.axis_index("zl"), lax.axis_index("zh"), lax.axis_index("c")
    near = lax.rem(zh + 3 + 2 * zl, 4)
    far = lax.rem(zh + 5 - 2 * zl, 4)
    opposite = lax.rem(zh + 2, 4)
    places = [zh * (2 * rows)]
    for block in (near, far, opposite):
        places.append(block * (2 * rows) + c * rows)
        places.append(block * (2 * rows) + (1 - c) * rows)
    return [pl.multiple_of(p, rows) for p in places]


def weight_product(xs, pieces):
    places = piece_places(pieces[1].shape[0])
    for place, w in zip(places, pieces):
        depth = w.shape[0]
        yield pl.ds(place, depth), dot(jnp.concatenate([x[:, pl.ds(place, depth)] for x in xs], axis=0), w[...])


def forward_kernel(x0, x1, x3, w0, a, a2, b, b2, d, d2, parts, whole, acc):
    tokens = x0.shape[0]
    pieces = (w0, a, a2, b, b2, d, d2)
    for w, (rows, term) in zip(pieces, weight_product((x0, x1, x3), pieces)):
        whole[rows, :] = w[...]
        if w is w0:
            acc[...] = term
        else:
            acc[...] += term
    me = lax.axis_index("x")
    for i, k in enumerate((0, 1, 3)):
        parts[lax.rem(me + 4 - k, 4)] = acc[i * tokens : (i + 1) * tokens, :].astype(BF16)


def last_forward_kernel(x2, w0, a, a2, b, b2, d, d2, begun, parts):
    opposite = lax.rem(lax.axis_index("x") + 2, 4)
    total = sum(term for _, term in weight_product((x2,), (w0, a, a2, b, b2, d, d2)))
    parts[...] = begun[...]
    parts[opposite] = total.astype(BF16)


def attention_kernel(parts, seg_ref, cot_ref, out):
    total = sum(parts[k].astype(F32) for k in range(4))
    projected = total.astype(BF16)
    count = projected.shape[0]
    heads = cot_ref.shape[1] // HD
    row = jnp.broadcast_to(seg_ref[...], (count, count))
    col = row.T
    here = lax.broadcasted_iota(jnp.int32, (count, count), 0)
    there = lax.broadcasted_iota(jnp.int32, (count, count), 1)
    allowed = (here >= there) & (row == col)
    keys = projected[:, heads * HD : (heads + 1) * HD]
    vals = projected[:, (heads + 1) * HD :]
    scale = 1.0 / math.sqrt(HD)
    grad_k = jnp.zeros((count, HD), F32)
    grad_v = jnp.zeros((count, HD), F32)
    for h in range(heads):
        query = projected[:, h * HD : (h + 1) * HD]
        cot = cot_ref[:, h * HD : (h + 1) * HD]
        scores = dot(query, keys, NT) * scale
        scores = jnp.where(allowed, scores, 0.0)
        weights = jnp.where(allowed, jnp.exp(scores), 0.0)
        weights = weights / jnp.sum(weights, axis=1, keepdims=True)
        grad_w = dot(cot, vals, NT)
        lean = jnp.sum(weights * grad_w, axis=1, keepdims=True)
        grad_s = (weights * (grad_w - lean) * scale).astype(BF16)
        out[:, h * HD : (h + 1) * HD] = dot(grad_s, keys).astype(BF16)
        grad_k += dot(grad_s, query, TN)
        grad_v += dot(weights.astype(BF16), cot, TN)
    out[:, heads * HD : (heads + 1) * HD] = grad_k.astype(BF16)
    out[:, (heads + 1) * HD :] = grad_v.astype(BF16)


def relative(g):
    n = g.shape[0]
    me = lax.axis_index("x")
    return jnp.concatenate([g[lax.rem(me + n - k, n)] for k in range(n)], axis=0)


def weight_terms(g, xs, core, shape):
    pieces, span, block = shape
    cols = g.shape[2]
    place = lax.broadcasted_iota(jnp.int32, (cols // 2, cols), 0)
    source = lax.broadcasted_iota(jnp.int32, (cols // 2, cols), 1)
    wanted = (place // span * 2 + core) * span + place % span
    pick = jnp.where(source == wanted, 1.0, 0.0).astype(BF16)
    left = dot(pick, relative(g), NT).astype(BF16)
    tile = 256
    for zh in range(4):
        for at in range(0, block, tile):
            start = zh * block + at
            term = dot(left, jnp.concatenate([r[:, start : start + tile] for r in xs], axis=0))
            for k in range(pieces // 4):
                yield (k * 4 + zh, slice(None), slice(at, at + tile)), term[k * span : (k + 1) * span]


def other_kernel(g, x0, x1, x2, x3, out):
    for at, piece in weight_terms(g, (x0, x1, x2, x3), 1 - lax.axis_index("c"), out.shape):
        out[at] = piece.astype(BF16)


def mine_kernel(g, x0, x1, x2, x3, got, out):
    for at, piece in weight_terms(g, (x0, x1, x2, x3), lax.axis_index("c"), out.shape):
        out[at] = (piece + got[at].astype(F32)).astype(BF16)


def input_kernel(g, whole, *outs):
    n, tokens, _ = g.shape
    grads = relative(g)
    tile = 256
    for at in range(0, whole.shape[0], tile):
        term = dot(grads, whole[at : at + tile, :], NT).astype(BF16)
        for k, out in enumerate(outs):
            out[:, at : at + tile] = term[k * tokens : (k + 1) * tokens]


def total_kernel(ref, out):
    out[...] = jnp.sum(ref[...].astype(F32), axis=0)


def shift(value, axis, k):
    n = lax.axis_size(axis)
    return lax.ppermute(value, axis, [(i, (i + k) % n) for i in range(n)])


def swap(value, axes):
    return lax.all_to_all(value, axes, 0, 0, tiled=True)


def z_move(value, target):
    pairs = []
    for zl in range(2):
        for zh in range(4):
            to_l, to_h = target(zl, zh)
            pairs.append((zl * 4 + zh, to_l * 4 + to_h % 4))
    return lax.ppermute(value, ("zl", "zh"), pairs)


def across(value):
    return z_move(value, lambda zl, zh: (0, zh + 1) if zl else (1, zh - 1))


def over(value):
    return z_move(value, lambda zl, zh: (zl, zh - 1 if zl else zh + 1))


def beside(value):
    return z_move(value, lambda zl, zh: (1 - zl, zh))


def on_device(inputs, segment_ids, qkv_weight, attn_cotangent):
    tokens, features = inputs.shape
    block, cols = qkv_weight.shape
    n = 4
    width = features // n
    half = block // 2
    span = cols // 32
    c = lax.axis_index("c")

    me = lax.axis_index("x")
    sent = [lax.dynamic_slice_in_dim(inputs, lax.rem(me + k, n) * width, width, 1) for k in range(n)]
    own = lax.dynamic_slice_in_dim(qkv_weight, c * half, half, 0)
    a = across(own)
    x1 = shift(sent[1], "x", 1)
    x3 = shift(sent[3], "x", 3)
    x1, x3, opposite = lax.optimization_barrier((x1, x3, sent[2]))
    x2 = shift(opposite, "x", 2)
    a2 = shift(a, "c", 1)
    b = beside(a)
    b2 = shift(b, "c", 1)
    d = over(a)
    d2 = shift(d, "c", 1)
    xs = (sent[0], x1, x2, x3)
    weights = (qkv_weight, a, a2, b, b2, d, d2)

    flops = 2 * n * tokens * width * cols
    begun, whole = pl.pallas_call(
        forward_kernel,
        out_shape=[arr((n, tokens, cols)), arr((width, cols))],
        scratch_shapes=[pltpu.VMEM(((n - 1) * tokens, cols), F32)],
        compiler_params=PARAMS,
        cost_estimate=cost(flops * 3 // 4, 6 << 20),
        name="forward",
    )(sent[0], x1, x3, *weights)
    parts = pl.pallas_call(
        last_forward_kernel,
        out_shape=arr((n, tokens, cols)),
        compiler_params=PARAMS,
        cost_estimate=cost(flops // 4, 5 << 20),
        name="last_forward",
    )(x2, *weights, begun)
    parts = swap(parts, "x")

    grads = pl.pallas_call(
        attention_kernel,
        out_shape=arr((tokens, cols)),
        compiler_params=PARAMS,
        cost_estimate=cost(1 << 28, 1 << 20),
        name="attention",
    )(parts, segment_ids, attn_cotangent)
    grads = lax.all_gather(grads, "x", axis=0, tiled=False)

    share = arr((64, span, block))
    other = pl.pallas_call(
        other_kernel,
        out_shape=share,
        compiler_params=PARAMS,
        cost_estimate=cost(flops // 2, 4 << 20),
        name="weight_grad_other_core",
    )(grads, *xs)
    got = shift(other, "c", 1)

    back = pl.pallas_call(
        input_kernel,
        out_shape=[arr((tokens, width))] * n,
        compiler_params=PARAMS,
        cost_estimate=cost(flops, 6 << 20),
        name="input_grad",
    )(grads, whole)
    got, back = lax.optimization_barrier((got, back))
    home = [back[0]] + [shift(back[k], "x", n - k) for k in range(1, n)]

    summed = pl.pallas_call(
        mine_kernel,
        out_shape=share,
        compiler_params=PARAMS,
        cost_estimate=cost(flops // 2, 6 << 20),
        name="weight_grad_this_core",
    )(grads, *xs, got)
    pieces = swap(summed, ("zl", "y", "zh"))
    weight_grad = pl.pallas_call(
        total_kernel,
        out_shape=arr((span, block), F32),
        compiler_params=PARAMS,
        cost_estimate=cost(1 << 20, 2 << 20),
        name="add_replicas",
    )(pieces).T

    input_grad = pl.pallas_call(
        join_kernel,
        out_shape=arr((tokens, features)),
        compiler_params=PARAMS,
        cost_estimate=cost(1 << 20, 4 << 20),
        name="join_features",
    )(*home)
    return (input_grad, weight_grad)


def solution(mesh):
    outer, inner = ("zl", "y", "c"), ("x", "zh")
    fine = Mesh(mesh.devices.reshape(2, 8, 2, 4, 4), outer + inner)
    return jax.shard_map(
        on_device,
        mesh=fine,
        in_specs=(
            P(outer + inner, None),
            P(outer + inner, None),
            P(inner, None),
            P(outer + inner, None),
        ),
        out_specs=(P(outer + inner, None), P(inner, outer)),
        check_vma=False,
    )
```

```python
import math

import jax
import jax.numpy as jnp
from jax import lax
from jax.experimental import pallas as pl
from jax.experimental.pallas import tpu as pltpu
from jax.sharding import Mesh
from jax.sharding import PartitionSpec as P

HD = 128
BF16 = jnp.bfloat16
F32 = jnp.float32
PARAMS = pltpu.CompilerParams(vmem_limit_bytes=20 * 1024 * 1024)

NT = (((1,), (1,)), ((), ()))
TN = (((0,), (0,)), ((), ()))


def arr(shape, dtype=BF16):
    return jax.ShapeDtypeStruct(shape, dtype)


def cost(flops, nbytes):
    return pl.CostEstimate(flops=flops, bytes_accessed=nbytes, transcendentals=0)


def dot(a, b, dims=(((1,), (0,)), ((), ()))):
    return lax.dot_general(a, b, dims, preferred_element_type=F32)


def join_kernel(*refs):
    ins, out = refs[:-1], refs[-1]
    n = len(ins)
    width = ins[0].shape[1]
    me = lax.axis_index("x")
    for k in range(n):
        start = pl.multiple_of(lax.rem(me + k, n) * width, width)
        out[:, pl.ds(start, width)] = ins[k][...]


def piece_places(rows):
    zl, zh, c = lax.axis_index("zl"), lax.axis_index("zh"), lax.axis_index("c")
    near = lax.rem(zh + 3 + 2 * zl, 4)
    far = lax.rem(zh + 5 - 2 * zl, 4)
    opposite = lax.rem(zh + 2, 4)
    places = [zh * (2 * rows)]
    for block in (near, far, opposite):
        places.append(block * (2 * rows) + c * rows)
        places.append(block * (2 * rows) + (1 - c) * rows)
    return [pl.multiple_of(p, rows) for p in places]


def weight_product(xs, place, w):
    return dot(jnp.concatenate([x[:, pl.ds(place, w.shape[0])] for x in xs], axis=0), w[...])


def forward_kernel(x0, x1, x2, x3, w0, a, a2, b, d, d2, whole, acc):
    places = piece_places(a.shape[0])
    for i, w in ((0, w0), (1, a), (2, a2), (3, b), (5, d), (6, d2)):
        whole[pl.ds(places[i], w.shape[0]), :] = w[...]
        term = weight_product((x0, x1, x2, x3), places[i], w)
        if w is w0:
            acc[...] = term
        else:
            acc[...] += term


def last_forward_kernel(x0, x1, x2, x3, b2, acc, parts):
    tokens = x0.shape[0]
    me = lax.axis_index("x")
    total = acc[...] + weight_product((x0, x1, x2, x3), piece_places(b2.shape[0])[4], b2)
    for k in range(4):
        parts[lax.rem(me + 4 - k, 4)] = total[k * tokens : (k + 1) * tokens, :].astype(BF16)


def attention_kernel(parts, seg_ref, cot_ref, out):
    total = sum(parts[k].astype(F32) for k in range(4))
    projected = total.astype(BF16)
    count = projected.shape[0]
    heads = cot_ref.shape[1] // HD
    row = jnp.broadcast_to(seg_ref[...], (count, count))
    col = row.T
    here = lax.broadcasted_iota(jnp.int32, (count, count), 0)
    there = lax.broadcasted_iota(jnp.int32, (count, count), 1)
    allowed = (here >= there) & (row == col)
    keys = projected[:, heads * HD : (heads + 1) * HD]
    vals = projected[:, (heads + 1) * HD :]
    scale = 1.0 / math.sqrt(HD)
    grad_k = jnp.zeros((count, HD), F32)
    grad_v = jnp.zeros((count, HD), F32)
    for h in range(heads):
        query = projected[:, h * HD : (h + 1) * HD]
        cot = cot_ref[:, h * HD : (h + 1) * HD]
        scores = dot(query, keys, NT) * scale
        scores = jnp.where(allowed, scores, 0.0)
        weights = jnp.where(allowed, jnp.exp(scores), 0.0)
        weights = weights / jnp.sum(weights, axis=1, keepdims=True)
        grad_w = dot(cot, vals, NT)
        lean = jnp.sum(weights * grad_w, axis=1, keepdims=True)
        grad_s = (weights * (grad_w - lean) * scale).astype(BF16)
        out[:, h * HD : (h + 1) * HD] = dot(grad_s, keys).astype(BF16)
        grad_k += dot(grad_s, query, TN)
        grad_v += dot(weights.astype(BF16), cot, TN)
    out[:, heads * HD : (heads + 1) * HD] = grad_k.astype(BF16)
    out[:, (heads + 1) * HD :] = grad_v.astype(BF16)


def relative(g):
    n = g.shape[0]
    me = lax.axis_index("x")
    return jnp.concatenate([g[lax.rem(me + n - k, n)] for k in range(n)], axis=0)


def weight_terms(g, xs, core, shape):
    pieces, span, block = shape
    cols = g.shape[2]
    place = lax.broadcasted_iota(jnp.int32, (cols // 2, cols), 0)
    source = lax.broadcasted_iota(jnp.int32, (cols // 2, cols), 1)
    wanted = (place // span * 2 + core) * span + place % span
    pick = jnp.where(source == wanted, 1.0, 0.0).astype(BF16)
    left = dot(pick, relative(g), NT).astype(BF16)
    tile = 256
    for zh in range(4):
        for at in range(0, block, tile):
            start = zh * block + at
            term = dot(left, jnp.concatenate([r[:, start : start + tile] for r in xs], axis=0))
            for k in range(pieces // 4):
                yield (k * 4 + zh, slice(None), slice(at, at + tile)), term[k * span : (k + 1) * span]


def other_kernel(g, x0, x1, x2, x3, out):
    for at, piece in weight_terms(g, (x0, x1, x2, x3), 1 - lax.axis_index("c"), out.shape):
        out[at] = piece.astype(BF16)


def mine_kernel(g, x0, x1, x2, x3, out):
    for at, piece in weight_terms(g, (x0, x1, x2, x3), lax.axis_index("c"), out.shape):
        out[at] = piece


def add_kernel(mine, got, out):
    out[...] = (mine[...] + got[...].astype(F32)).astype(BF16)


def input_kernel(g, whole, b2, *outs):
    tokens = g.shape[1]
    tile = b2.shape[0]
    grads = relative(g)
    pieces = [(at, whole[at : at + tile, :]) for at in range(0, whole.shape[0], tile)]
    pieces.append((piece_places(tile)[4], b2[...]))
    for at, w in pieces:
        term = dot(grads, w, NT).astype(BF16)
        for k, out in enumerate(outs):
            out[:, pl.ds(at, tile)] = term[k * tokens : (k + 1) * tokens]


def total_kernel(ref, out):
    out[...] = jnp.sum(ref[...].astype(F32), axis=0)


def shift(value, axis, k):
    n = lax.axis_size(axis)
    return lax.ppermute(value, axis, [(i, (i + k) % n) for i in range(n)])


def swap(value, axes):
    return lax.all_to_all(value, axes, 0, 0, tiled=True)


def z_move(value, target):
    pairs = []
    for zl in range(2):
        for zh in range(4):
            to_l, to_h = target(zl, zh)
            pairs.append((zl * 4 + zh, to_l * 4 + to_h % 4))
    return lax.ppermute(value, ("zl", "zh"), pairs)


def across(value):
    return z_move(value, lambda zl, zh: (0, zh + 1) if zl else (1, zh - 1))


def over(value):
    return z_move(value, lambda zl, zh: (zl, zh - 1 if zl else zh + 1))


def beside(value):
    return z_move(value, lambda zl, zh: (1 - zl, zh))


def on_device(inputs, segment_ids, qkv_weight, attn_cotangent):
    tokens, features = inputs.shape
    block, cols = qkv_weight.shape
    n = 4
    width = features // n
    half = block // 2
    span = cols // 32
    c = lax.axis_index("c")

    me = lax.axis_index("x")
    sent = [lax.dynamic_slice_in_dim(inputs, lax.rem(me + k, n) * width, width, 1) for k in range(n)]
    own = lax.dynamic_slice_in_dim(qkv_weight, c * half, half, 0)
    a = across(own)
    x2 = shift(sent[2], "x", 2)
    x2, ahead, behind = lax.optimization_barrier((x2, sent[1], sent[3]))
    x1 = shift(ahead, "x", 1)
    x3 = shift(behind, "x", 3)
    a2 = shift(a, "c", 1)
    b = beside(a)
    b2 = shift(b, "c", 1)
    d = over(a)
    d2 = shift(d, "c", 1)
    xs = (sent[0], x1, x2, x3)

    flops = 2 * n * tokens * width * cols
    whole, begun = pl.pallas_call(
        forward_kernel,
        out_shape=[arr((width, cols)), arr((n * tokens, cols), F32)],
        compiler_params=PARAMS,
        cost_estimate=cost(flops, 8 << 20),
        name="forward",
    )(*xs, qkv_weight, a, a2, b, d, d2)
    parts = pl.pallas_call(
        last_forward_kernel,
        out_shape=arr((n, tokens, cols)),
        compiler_params=PARAMS,
        cost_estimate=cost(flops // 8, 3 << 20),
        name="last_forward",
    )(*xs, b2, begun)
    parts = swap(parts, "x")

    grads = pl.pallas_call(
        attention_kernel,
        out_shape=arr((tokens, cols)),
        compiler_params=PARAMS,
        cost_estimate=cost(1 << 28, 1 << 20),
        name="attention",
    )(parts, segment_ids, attn_cotangent)
    grads = lax.all_gather(grads, "x", axis=0, tiled=False)

    share = arr((64, span, block))
    other = pl.pallas_call(
        other_kernel,
        out_shape=share,
        compiler_params=PARAMS,
        cost_estimate=cost(flops // 2, 4 << 20),
        name="weight_grad_other_core",
    )(grads, *xs)
    got = shift(other, "c", 1)

    back = pl.pallas_call(
        input_kernel,
        out_shape=[arr((tokens, width))] * n,
        compiler_params=PARAMS,
        cost_estimate=cost(flops, 6 << 20),
        name="input_grad",
    )(grads, whole, b2)
    got, back = lax.optimization_barrier((got, back))
    home = [back[0]] + [shift(back[k], "x", n - k) for k in range(1, n)]

    mine = pl.pallas_call(
        mine_kernel,
        out_shape=arr(share.shape, F32),
        compiler_params=PARAMS,
        cost_estimate=cost(flops // 2, 6 << 20),
        name="weight_grad_this_core",
    )(grads, *xs)
    summed = pl.pallas_call(
        add_kernel,
        out_shape=share,
        compiler_params=PARAMS,
        cost_estimate=cost(1 << 20, 6 << 20),
        name="add_cores",
    )(mine, got)
    pieces = swap(summed, ("zl", "y", "zh"))
    weight_grad = pl.pallas_call(
        total_kernel,
        out_shape=arr((span, block), F32),
        compiler_params=PARAMS,
        cost_estimate=cost(1 << 20, 2 << 20),
        name="add_replicas",
    )(pieces).T

    input_grad = pl.pallas_call(
        join_kernel,
        out_shape=arr((tokens, features)),
        compiler_params=PARAMS,
        cost_estimate=cost(1 << 20, 4 << 20),
        name="join_features",
    )(*home)
    return (input_grad, weight_grad)


def solution(mesh):
    outer, inner = ("zl", "y", "c"), ("x", "zh")
    fine = Mesh(mesh.devices.reshape(2, 8, 2, 4, 4), outer + inner)
    return jax.shard_map(
        on_device,
        mesh=fine,
        in_specs=(
            P(outer + inner, None),
            P(outer + inner, None),
            P(inner, None),
            P(outer + inner, None),
        ),
        out_specs=(P(outer + inner, None), P(inner, outer)),
        check_vma=False,
    )
```

```python
import math

import jax
import jax.numpy as jnp
from jax import lax
from jax.experimental import pallas as pl
from jax.experimental.pallas import tpu as pltpu
from jax.sharding import Mesh
from jax.sharding import PartitionSpec as P

HD = 128
BF16 = jnp.bfloat16
F32 = jnp.float32
PARAMS = pltpu.CompilerParams(vmem_limit_bytes=20 * 1024 * 1024)

NT = (((1,), (1,)), ((), ()))
TN = (((0,), (0,)), ((), ()))


def arr(shape, dtype=BF16):
    return jax.ShapeDtypeStruct(shape, dtype)


def cost(flops, nbytes):
    return pl.CostEstimate(flops=flops, bytes_accessed=nbytes, transcendentals=0)


def dot(a, b, dims=(((1,), (0,)), ((), ()))):
    return lax.dot_general(a, b, dims, preferred_element_type=F32)


def join_kernel(*refs):
    ins, out = refs[:-1], refs[-1]
    n = len(ins)
    width = ins[0].shape[1]
    me = lax.axis_index("x")
    for k in range(n):
        start = pl.multiple_of(lax.rem(me + k, n) * width, width)
        out[:, pl.ds(start, width)] = ins[k][...]


def piece_places(rows):
    zl, zh, c = lax.axis_index("zl"), lax.axis_index("zh"), lax.axis_index("c")
    near = lax.rem(zh + 3 + 2 * zl, 4)
    far = lax.rem(zh + 5 - 2 * zl, 4)
    opposite = lax.rem(zh + 2, 4)
    places = [zh * (2 * rows)]
    for block in (near, far, opposite):
        places.append(block * (2 * rows) + c * rows)
        places.append(block * (2 * rows) + (1 - c) * rows)
    return [pl.multiple_of(p, rows) for p in places]


def weight_product(xs, place, w):
    return dot(jnp.concatenate([x[:, pl.ds(place, w.shape[0])] for x in xs], axis=0), w[...])


def forward_kernel(x0, x1, x2, w0, a, a2, b, d, d2, whole, acc):
    places = piece_places(a.shape[0])
    for i, w in ((0, w0), (1, a), (2, a2), (3, b), (5, d), (6, d2)):
        whole[pl.ds(places[i], w.shape[0]), :] = w[...]
        term = weight_product((x0, x1, x2), places[i], w)
        if w is w0:
            acc[...] = term
        else:
            acc[...] += term


def last_forward_kernel(x0, x1, x2, x3, w0, a, a2, b, b2, d, d2, acc, parts):
    tokens = x0.shape[0]
    me = lax.axis_index("x")
    places = piece_places(a.shape[0])
    total = acc[...] + weight_product((x0, x1, x2), places[4], b2)
    for k in range(3):
        parts[lax.rem(me + 4 - k, 4)] = total[k * tokens : (k + 1) * tokens, :].astype(BF16)
    total = sum(weight_product((x3,), place, w) for place, w in zip(places, (w0, a, a2, b, b2, d, d2)))
    parts[lax.rem(me + 1, 4)] = total.astype(BF16)


def attention_kernel(parts, seg_ref, cot_ref, out):
    total = sum(parts[k].astype(F32) for k in range(4))
    projected = total.astype(BF16)
    count = projected.shape[0]
    heads = cot_ref.shape[1] // HD
    row = jnp.broadcast_to(seg_ref[...], (count, count))
    col = row.T
    here = lax.broadcasted_iota(jnp.int32, (count, count), 0)
    there = lax.broadcasted_iota(jnp.int32, (count, count), 1)
    allowed = (here >= there) & (row == col)
    keys = projected[:, heads * HD : (heads + 1) * HD]
    vals = projected[:, (heads + 1) * HD :]
    scale = 1.0 / math.sqrt(HD)
    grad_k = jnp.zeros((count, HD), F32)
    grad_v = jnp.zeros((count, HD), F32)
    for h in range(heads):
        query = projected[:, h * HD : (h + 1) * HD]
        cot = cot_ref[:, h * HD : (h + 1) * HD]
        scores = dot(query, keys, NT) * scale
        scores = jnp.where(allowed, scores, 0.0)
        weights = jnp.where(allowed, jnp.exp(scores), 0.0)
        weights = weights / jnp.sum(weights, axis=1, keepdims=True)
        grad_w = dot(cot, vals, NT)
        lean = jnp.sum(weights * grad_w, axis=1, keepdims=True)
        grad_s = (weights * (grad_w - lean) * scale).astype(BF16)
        out[:, h * HD : (h + 1) * HD] = dot(grad_s, keys).astype(BF16)
        grad_k += dot(grad_s, query, TN)
        grad_v += dot(weights.astype(BF16), cot, TN)
    out[:, heads * HD : (heads + 1) * HD] = grad_k.astype(BF16)
    out[:, (heads + 1) * HD :] = grad_v.astype(BF16)


def relative(g):
    n = g.shape[0]
    me = lax.axis_index("x")
    return jnp.concatenate([g[lax.rem(me + n - k, n)] for k in range(n)], axis=0)


def weight_terms(g, xs, core, shape):
    pieces, span, block = shape
    cols = g.shape[2]
    place = lax.broadcasted_iota(jnp.int32, (cols // 2, cols), 0)
    source = lax.broadcasted_iota(jnp.int32, (cols // 2, cols), 1)
    wanted = (place // span * 2 + core) * span + place % span
    pick = jnp.where(source == wanted, 1.0, 0.0).astype(BF16)
    left = dot(pick, relative(g), NT).astype(BF16)
    tile = 256
    for zh in range(4):
        for at in range(0, block, tile):
            start = zh * block + at
            term = dot(left, jnp.concatenate([r[:, start : start + tile] for r in xs], axis=0))
            for k in range(pieces // 4):
                yield (k * 4 + zh, slice(None), slice(at, at + tile)), term[k * span : (k + 1) * span]


def other_kernel(g, x0, x1, x2, x3, out):
    for at, piece in weight_terms(g, (x0, x1, x2, x3), 1 - lax.axis_index("c"), out.shape):
        out[at] = piece.astype(BF16)


def mine_kernel(g, x0, x1, x2, x3, out):
    for at, piece in weight_terms(g, (x0, x1, x2, x3), lax.axis_index("c"), out.shape):
        out[at] = piece


def add_kernel(mine, got, out):
    out[...] = (mine[...] + got[...].astype(F32)).astype(BF16)


def input_kernel(g, whole, b2, *outs):
    tokens = g.shape[1]
    tile = b2.shape[0]
    grads = relative(g)
    pieces = [(at, whole[at : at + tile, :]) for at in range(0, whole.shape[0], tile)]
    pieces.append((piece_places(tile)[4], b2[...]))
    for at, w in pieces:
        term = dot(grads, w, NT).astype(BF16)
        for k, out in enumerate(outs):
            out[:, pl.ds(at, tile)] = term[k * tokens : (k + 1) * tokens]


def total_kernel(ref, out):
    out[...] = jnp.sum(ref[...].astype(F32), axis=0)


def shift(value, axis, k):
    n = lax.axis_size(axis)
    return lax.ppermute(value, axis, [(i, (i + k) % n) for i in range(n)])


def swap(value, axes):
    return lax.all_to_all(value, axes, 0, 0, tiled=True)


def z_move(value, target):
    pairs = []
    for zl in range(2):
        for zh in range(4):
            to_l, to_h = target(zl, zh)
            pairs.append((zl * 4 + zh, to_l * 4 + to_h % 4))
    return lax.ppermute(value, ("zl", "zh"), pairs)


def across(value):
    return z_move(value, lambda zl, zh: (0, zh + 1) if zl else (1, zh - 1))


def over(value):
    return z_move(value, lambda zl, zh: (zl, zh - 1 if zl else zh + 1))


def beside(value):
    return z_move(value, lambda zl, zh: (1 - zl, zh))


def on_device(inputs, segment_ids, qkv_weight, attn_cotangent):
    tokens, features = inputs.shape
    block, cols = qkv_weight.shape
    n = 4
    width = features // n
    half = block // 2
    span = cols // 32
    c = lax.axis_index("c")

    me = lax.axis_index("x")
    sent = [lax.dynamic_slice_in_dim(inputs, lax.rem(me + k, n) * width, width, 1) for k in range(n)]
    own = lax.dynamic_slice_in_dim(qkv_weight, c * half, half, 0)
    a = across(own)
    x2 = shift(sent[2], "x", 2)
    x2, ahead, behind = lax.optimization_barrier((x2, sent[1], sent[3]))
    x1 = shift(ahead, "x", 1)
    x3 = shift(behind, "x", 3)
    a2 = shift(a, "c", 1)
    b = beside(a)
    b2 = shift(b, "c", 1)
    d = over(a)
    d2 = shift(d, "c", 1)
    xs = (sent[0], x1, x2, x3)

    flops = 2 * n * tokens * width * cols
    whole, begun = pl.pallas_call(
        forward_kernel,
        out_shape=[arr((width, cols)), arr(((n - 1) * tokens, cols), F32)],
        compiler_params=PARAMS,
        cost_estimate=cost(flops * 3 // 4, 8 << 20),
        name="forward",
    )(*xs[:3], qkv_weight, a, a2, b, d, d2)
    parts = pl.pallas_call(
        last_forward_kernel,
        out_shape=arr((n, tokens, cols)),
        compiler_params=PARAMS,
        cost_estimate=cost(flops // 4, 5 << 20),
        name="last_forward",
    )(*xs, qkv_weight, a, a2, b, b2, d, d2, begun)
    parts = swap(parts, "x")

    grads = pl.pallas_call(
        attention_kernel,
        out_shape=arr((tokens, cols)),
        compiler_params=PARAMS,
        cost_estimate=cost(1 << 28, 1 << 20),
        name="attention",
    )(parts, segment_ids, attn_cotangent)
    grads = lax.all_gather(grads, "x", axis=0, tiled=False)

    share = arr((64, span, block))
    other = pl.pallas_call(
        other_kernel,
        out_shape=share,
        compiler_params=PARAMS,
        cost_estimate=cost(flops // 2, 4 << 20),
        name="weight_grad_other_core",
    )(grads, *xs)
    got = shift(other, "c", 1)

    back = pl.pallas_call(
        input_kernel,
        out_shape=[arr((tokens, width))] * n,
        compiler_params=PARAMS,
        cost_estimate=cost(flops, 6 << 20),
        name="input_grad",
    )(grads, whole, b2)
    got, back = lax.optimization_barrier((got, back))
    home = [back[0]] + [shift(back[k], "x", n - k) for k in range(1, n)]

    mine = pl.pallas_call(
        mine_kernel,
        out_shape=arr(share.shape, F32),
        compiler_params=PARAMS,
        cost_estimate=cost(flops // 2, 6 << 20),
        name="weight_grad_this_core",
    )(grads, *xs)
    summed = pl.pallas_call(
        add_kernel,
        out_shape=share,
        compiler_params=PARAMS,
        cost_estimate=cost(1 << 20, 6 << 20),
        name="add_cores",
    )(mine, got)
    pieces = swap(summed, ("zl", "y", "zh"))
    weight_grad = pl.pallas_call(
        total_kernel,
        out_shape=arr((span, block), F32),
        compiler_params=PARAMS,
        cost_estimate=cost(1 << 20, 2 << 20),
        name="add_replicas",
    )(pieces).T

    input_grad = pl.pallas_call(
        join_kernel,
        out_shape=arr((tokens, features)),
        compiler_params=PARAMS,
        cost_estimate=cost(1 << 20, 4 << 20),
        name="join_features",
    )(*home)
    return (input_grad, weight_grad)


def solution(mesh):
    outer, inner = ("zl", "y", "c"), ("x", "zh")
    fine = Mesh(mesh.devices.reshape(2, 8, 2, 4, 4), outer + inner)
    return jax.shard_map(
        on_device,
        mesh=fine,
        in_specs=(
            P(outer + inner, None),
            P(outer + inner, None),
            P(inner, None),
            P(outer + inner, None),
        ),
        out_specs=(P(outer + inner, None), P(inner, outer)),
        check_vma=False,
    )
```

```python
import math

import jax
import jax.numpy as jnp
from jax import lax
from jax.experimental import pallas as pl
from jax.experimental.pallas import tpu as pltpu
from jax.sharding import Mesh
from jax.sharding import PartitionSpec as P

HD = 128
BF16 = jnp.bfloat16
F32 = jnp.float32
PARAMS = pltpu.CompilerParams(vmem_limit_bytes=20 * 1024 * 1024)

NT = (((1,), (1,)), ((), ()))
TN = (((0,), (0,)), ((), ()))


def arr(shape, dtype=BF16):
    return jax.ShapeDtypeStruct(shape, dtype)


def cost(flops, nbytes):
    return pl.CostEstimate(flops=flops, bytes_accessed=nbytes, transcendentals=0)


def dot(a, b, dims=(((1,), (0,)), ((), ()))):
    return lax.dot_general(a, b, dims, preferred_element_type=F32)


def join_kernel(*refs):
    ins, out = refs[:-1], refs[-1]
    n = len(ins)
    width = ins[0].shape[1]
    me = lax.axis_index("x")
    for k in range(n):
        start = pl.multiple_of(lax.rem(me + k, n) * width, width)
        out[:, pl.ds(start, width)] = ins[k][...]


def piece_places(rows):
    zl, zh, c = lax.axis_index("zl"), lax.axis_index("zh"), lax.axis_index("c")
    near = lax.rem(zh + 3 + 2 * zl, 4)
    far = lax.rem(zh + 5 - 2 * zl, 4)
    opposite = lax.rem(zh + 2, 4)
    places = [zh * (2 * rows)]
    for block in (near, far, opposite):
        places.append(block * (2 * rows) + c * rows)
        places.append(block * (2 * rows) + (1 - c) * rows)
    return [pl.multiple_of(p, rows) for p in places]


def weight_product(xs, place, w):
    return dot(jnp.concatenate([x[:, pl.ds(place, w.shape[0])] for x in xs], axis=0), w[...])


def forward_kernel(x0, x1, x2, w0, a, a2, b, d, d2, whole, acc):
    places = piece_places(a.shape[0])
    for i, w in ((0, w0), (1, a), (2, a2), (3, b), (5, d), (6, d2)):
        whole[pl.ds(places[i], w.shape[0]), :] = w[...]
        term = weight_product((x0, x1, x2), places[i], w)
        if w is w0:
            acc[...] = term
        else:
            acc[...] += term


def last_forward_kernel(x0, x1, x2, x3, w0, a, a2, b, b2, d, d2, acc, parts):
    tokens = x0.shape[0]
    me = lax.axis_index("x")
    places = piece_places(a.shape[0])
    total = acc[...] + weight_product((x0, x1, x2), places[4], b2)
    for k in range(3):
        parts[lax.rem(me + 4 - k, 4)] = total[k * tokens : (k + 1) * tokens, :].astype(BF16)
    total = sum(weight_product((x3,), place, w) for place, w in zip(places, (w0, a, a2, b, b2, d, d2)))
    parts[lax.rem(me + 1, 4)] = total.astype(BF16)


def attention_kernel(parts, seg_ref, cot_ref, out):
    total = sum(parts[k].astype(F32) for k in range(4))
    projected = total.astype(BF16)
    count = projected.shape[0]
    heads = cot_ref.shape[1] // HD
    row = jnp.broadcast_to(seg_ref[...], (count, count))
    col = row.T
    here = lax.broadcasted_iota(jnp.int32, (count, count), 0)
    there = lax.broadcasted_iota(jnp.int32, (count, count), 1)
    allowed = (here >= there) & (row == col)
    keys = projected[:, heads * HD : (heads + 1) * HD]
    vals = projected[:, (heads + 1) * HD :]
    scale = 1.0 / math.sqrt(HD)
    grad_k = jnp.zeros((count, HD), F32)
    grad_v = jnp.zeros((count, HD), F32)
    for h in range(heads):
        query = projected[:, h * HD : (h + 1) * HD]
        cot = cot_ref[:, h * HD : (h + 1) * HD]
        scores = dot(query, keys, NT) * scale
        scores = jnp.where(allowed, scores, 0.0)
        weights = jnp.where(allowed, jnp.exp(scores), 0.0)
        weights = weights / jnp.sum(weights, axis=1, keepdims=True)
        grad_w = dot(cot, vals, NT)
        lean = jnp.sum(weights * grad_w, axis=1, keepdims=True)
        grad_s = (weights * (grad_w - lean) * scale).astype(BF16)
        out[:, h * HD : (h + 1) * HD] = dot(grad_s, keys).astype(BF16)
        grad_k += dot(grad_s, query, TN)
        grad_v += dot(weights.astype(BF16), cot, TN)
    out[:, heads * HD : (heads + 1) * HD] = grad_k.astype(BF16)
    out[:, (heads + 1) * HD :] = grad_v.astype(BF16)


def relative(g):
    n = g.shape[0]
    me = lax.axis_index("x")
    return jnp.concatenate([g[lax.rem(me + n - k, n)] for k in range(n)], axis=0)


def weight_terms(g, xs, core, shape):
    pieces, span, block = shape
    cols = g.shape[2]
    place = lax.broadcasted_iota(jnp.int32, (cols // 2, cols), 0)
    source = lax.broadcasted_iota(jnp.int32, (cols // 2, cols), 1)
    wanted = (place // span * 2 + core) * span + place % span
    pick = jnp.where(source == wanted, 1.0, 0.0).astype(BF16)
    left = dot(pick, relative(g), NT).astype(BF16)
    tile = 256
    for zh in range(4):
        for at in range(0, block, tile):
            start = zh * block + at
            term = dot(left, jnp.concatenate([r[:, start : start + tile] for r in xs], axis=0))
            for k in range(pieces // 4):
                yield (k * 4 + zh, slice(None), slice(at, at + tile)), term[k * span : (k + 1) * span]


def other_kernel(g, x0, x1, x2, x3, out):
    for at, piece in weight_terms(g, (x0, x1, x2, x3), 1 - lax.axis_index("c"), out.shape):
        out[at] = piece.astype(BF16)


def mine_kernel(g, x0, x1, x2, x3, out):
    for at, piece in weight_terms(g, (x0, x1, x2, x3), lax.axis_index("c"), out.shape):
        out[at] = piece


def add_kernel(mine, got, out):
    out[...] = (mine[...] + got[...].astype(F32)).astype(BF16)


def input_kernel(g, whole, b2, *outs):
    tokens = g.shape[1]
    tile = b2.shape[0]
    grads = relative(g)
    pieces = [(at, whole[at : at + tile, :]) for at in range(0, whole.shape[0], tile)]
    pieces.append((piece_places(tile)[4], b2[...]))
    for at, w in pieces:
        term = dot(grads, w, NT).astype(BF16)
        for k, out in enumerate(outs):
            out[:, pl.ds(at, tile)] = term[k * tokens : (k + 1) * tokens]


def total_kernel(ref, out):
    out[...] = jnp.sum(ref[...].astype(F32), axis=0)


def shift(value, axis, k):
    n = lax.axis_size(axis)
    return lax.ppermute(value, axis, [(i, (i + k) % n) for i in range(n)])


def swap(value, axes):
    return lax.all_to_all(value, axes, 0, 0, tiled=True)


def z_move(value, target):
    pairs = []
    for zl in range(2):
        for zh in range(4):
            to_l, to_h = target(zl, zh)
            pairs.append((zl * 4 + zh, to_l * 4 + to_h % 4))
    return lax.ppermute(value, ("zl", "zh"), pairs)


def across(value):
    return z_move(value, lambda zl, zh: (0, zh + 1) if zl else (1, zh - 1))


def over(value):
    return z_move(value, lambda zl, zh: (zl, zh - 1 if zl else zh + 1))


def beside(value):
    return z_move(value, lambda zl, zh: (1 - zl, zh))


def on_device(inputs, segment_ids, qkv_weight, attn_cotangent):
    tokens, features = inputs.shape
    block, cols = qkv_weight.shape
    n = 4
    width = features // n
    half = block // 2
    span = cols // 32
    c = lax.axis_index("c")

    me = lax.axis_index("x")
    def cut(value, k):
        return lax.dynamic_slice_in_dim(value, lax.rem(me + k, n) * width, width, 1)

    opposite, rest = lax.optimization_barrier((cut(inputs, 2), inputs))
    sent = [cut(rest, 0), cut(rest, 1), opposite, cut(rest, 3)]
    own = lax.dynamic_slice_in_dim(qkv_weight, c * half, half, 0)
    a = across(own)
    x2 = shift(sent[2], "x", 2)
    x2, ahead, behind = lax.optimization_barrier((x2, sent[1], sent[3]))
    x1 = shift(ahead, "x", 1)
    x3 = shift(behind, "x", 3)
    a2 = shift(a, "c", 1)
    b = beside(a)
    b2 = shift(b, "c", 1)
    d = over(a)
    d2 = shift(d, "c", 1)
    xs = (sent[0], x1, x2, x3)

    flops = 2 * n * tokens * width * cols
    whole, begun = pl.pallas_call(
        forward_kernel,
        out_shape=[arr((width, cols)), arr(((n - 1) * tokens, cols), F32)],
        compiler_params=PARAMS,
        cost_estimate=cost(flops * 3 // 4, 8 << 20),
        name="forward",
    )(*xs[:3], qkv_weight, a, a2, b, d, d2)
    parts = pl.pallas_call(
        last_forward_kernel,
        out_shape=arr((n, tokens, cols)),
        compiler_params=PARAMS,
        cost_estimate=cost(flops // 4, 5 << 20),
        name="last_forward",
    )(*xs, qkv_weight, a, a2, b, b2, d, d2, begun)
    parts = swap(parts, "x")

    grads = pl.pallas_call(
        attention_kernel,
        out_shape=arr((tokens, cols)),
        compiler_params=PARAMS,
        cost_estimate=cost(1 << 28, 1 << 20),
        name="attention",
    )(parts, segment_ids, attn_cotangent)
    grads = lax.all_gather(grads, "x", axis=0, tiled=False)

    share = arr((64, span, block))
    other = pl.pallas_call(
        other_kernel,
        out_shape=share,
        compiler_params=PARAMS,
        cost_estimate=cost(flops // 2, 4 << 20),
        name="weight_grad_other_core",
    )(grads, *xs)
    got = shift(other, "c", 1)

    back = pl.pallas_call(
        input_kernel,
        out_shape=[arr((tokens, width))] * n,
        compiler_params=PARAMS,
        cost_estimate=cost(flops, 6 << 20),
        name="input_grad",
    )(grads, whole, b2)
    got, back = lax.optimization_barrier((got, back))
    home = [back[0]] + [shift(back[k], "x", n - k) for k in range(1, n)]

    mine = pl.pallas_call(
        mine_kernel,
        out_shape=arr(share.shape, F32),
        compiler_params=PARAMS,
        cost_estimate=cost(flops // 2, 6 << 20),
        name="weight_grad_this_core",
    )(grads, *xs)
    summed = pl.pallas_call(
        add_kernel,
        out_shape=share,
        compiler_params=PARAMS,
        cost_estimate=cost(1 << 20, 6 << 20),
        name="add_cores",
    )(mine, got)
    pieces = swap(summed, ("zl", "y", "zh"))
    weight_grad = pl.pallas_call(
        total_kernel,
        out_shape=arr((span, block), F32),
        compiler_params=PARAMS,
        cost_estimate=cost(1 << 20, 2 << 20),
        name="add_replicas",
    )(pieces).T

    input_grad = pl.pallas_call(
        join_kernel,
        out_shape=arr((tokens, features)),
        compiler_params=PARAMS,
        cost_estimate=cost(1 << 20, 4 << 20),
        name="join_features",
    )(*home)
    return (input_grad, weight_grad)


def solution(mesh):
    outer, inner = ("zl", "y", "c"), ("x", "zh")
    fine = Mesh(mesh.devices.reshape(2, 8, 2, 4, 4), outer + inner)
    return jax.shard_map(
        on_device,
        mesh=fine,
        in_specs=(
            P(outer + inner, None),
            P(outer + inner, None),
            P(inner, None),
            P(outer + inner, None),
        ),
        out_specs=(P(outer + inner, None), P(inner, outer)),
        check_vma=False,
    )
```

```python
import math

import jax
import jax.numpy as jnp
from jax import lax
from jax.experimental import pallas as pl
from jax.experimental.pallas import tpu as pltpu
from jax.sharding import Mesh
from jax.sharding import PartitionSpec as P

HD = 128
BF16 = jnp.bfloat16
F32 = jnp.float32
PARAMS = pltpu.CompilerParams(vmem_limit_bytes=20 * 1024 * 1024)

NT = (((1,), (1,)), ((), ()))
TN = (((0,), (0,)), ((), ()))


def arr(shape, dtype=BF16):
    return jax.ShapeDtypeStruct(shape, dtype)


def cost(flops, nbytes):
    return pl.CostEstimate(flops=flops, bytes_accessed=nbytes, transcendentals=0)


def dot(a, b, dims=(((1,), (0,)), ((), ()))):
    return lax.dot_general(a, b, dims, preferred_element_type=F32)


def join_kernel(*refs):
    ins, out = refs[:-1], refs[-1]
    n = len(ins)
    width = ins[0].shape[1]
    me = lax.axis_index("x")
    for k in range(n):
        start = pl.multiple_of(lax.rem(me + k, n) * width, width)
        out[:, pl.ds(start, width)] = ins[k][...]


def piece_places(rows):
    zl, zh, c = lax.axis_index("zl"), lax.axis_index("zh"), lax.axis_index("c")
    near = lax.rem(zh + 3 + 2 * zl, 4)
    far = lax.rem(zh + 5 - 2 * zl, 4)
    opposite = lax.rem(zh + 2, 4)
    places = [zh * (2 * rows)]
    for block in (near, far, opposite):
        places.append(block * (2 * rows) + c * rows)
        places.append(block * (2 * rows) + (1 - c) * rows)
    return [pl.multiple_of(p, rows) for p in places]


def weight_product(xs, place, w):
    return dot(jnp.concatenate([x[:, pl.ds(place, w.shape[0])] for x in xs], axis=0), w[...])


def forward_kernel(x0, x1, x2, w0, a, a2, b, d, d2, whole, acc):
    places = piece_places(a.shape[0])
    for i, w in ((0, w0), (1, a), (2, a2), (3, b), (5, d), (6, d2)):
        whole[pl.ds(places[i], w.shape[0]), :] = w[...]
        term = weight_product((x0, x1, x2), places[i], w)
        if w is w0:
            acc[...] = term
        else:
            acc[...] += term


def last_forward_kernel(x0, x1, x2, x3, w0, a, a2, b, b2, d, d2, acc, parts):
    tokens = x0.shape[0]
    me = lax.axis_index("x")
    places = piece_places(a.shape[0])
    total = acc[...] + weight_product((x0, x1, x2), places[4], b2)
    for k in range(3):
        parts[lax.rem(me + 4 - k, 4)] = total[k * tokens : (k + 1) * tokens, :].astype(BF16)
    total = sum(weight_product((x3,), place, w) for place, w in zip(places, (w0, a, a2, b, b2, d, d2)))
    parts[lax.rem(me + 1, 4)] = total.astype(BF16)


def attention_kernel(parts, seg_ref, cot_ref, out):
    total = sum(parts[k].astype(F32) for k in range(4))
    projected = total.astype(BF16)
    count = projected.shape[0]
    heads = cot_ref.shape[1] // HD
    row = jnp.broadcast_to(seg_ref[...], (count, count))
    col = row.T
    here = lax.broadcasted_iota(jnp.int32, (count, count), 0)
    there = lax.broadcasted_iota(jnp.int32, (count, count), 1)
    allowed = (here >= there) & (row == col)
    keys = projected[:, heads * HD : (heads + 1) * HD]
    vals = projected[:, (heads + 1) * HD :]
    scale = 1.0 / math.sqrt(HD)
    grad_k = jnp.zeros((count, HD), F32)
    grad_v = jnp.zeros((count, HD), F32)
    for h in range(heads):
        query = projected[:, h * HD : (h + 1) * HD]
        cot = cot_ref[:, h * HD : (h + 1) * HD]
        scores = dot(query, keys, NT) * scale
        scores = jnp.where(allowed, scores, 0.0)
        weights = jnp.where(allowed, jnp.exp(scores), 0.0)
        weights = weights / jnp.sum(weights, axis=1, keepdims=True)
        grad_w = dot(cot, vals, NT)
        lean = jnp.sum(weights * grad_w, axis=1, keepdims=True)
        grad_s = (weights * (grad_w - lean) * scale).astype(BF16)
        out[:, h * HD : (h + 1) * HD] = dot(grad_s, keys).astype(BF16)
        grad_k += dot(grad_s, query, TN)
        grad_v += dot(weights.astype(BF16), cot, TN)
    out[:, heads * HD : (heads + 1) * HD] = grad_k.astype(BF16)
    out[:, (heads + 1) * HD :] = grad_v.astype(BF16)


def relative(g):
    n = g.shape[0]
    me = lax.axis_index("x")
    return jnp.concatenate([g[lax.rem(me + n - k, n)] for k in range(n)], axis=0)


def weight_terms(g, xs, core, shape):
    pieces, span, block = shape
    cols = g.shape[2]
    place = lax.broadcasted_iota(jnp.int32, (cols // 2, cols), 0)
    source = lax.broadcasted_iota(jnp.int32, (cols // 2, cols), 1)
    wanted = (place // span * 2 + core) * span + place % span
    pick = jnp.where(source == wanted, 1.0, 0.0).astype(BF16)
    left = dot(pick, relative(g), NT).astype(BF16)
    tile = 256
    for zh in range(4):
        for at in range(0, block, tile):
            start = zh * block + at
            term = dot(left, jnp.concatenate([r[:, start : start + tile] for r in xs], axis=0))
            for k in range(pieces // 4):
                yield (k * 4 + zh, slice(None), slice(at, at + tile)), term[k * span : (k + 1) * span]


def other_kernel(g, x0, x1, x2, x3, out):
    for at, piece in weight_terms(g, (x0, x1, x2, x3), 1 - lax.axis_index("c"), out.shape):
        out[at] = piece.astype(BF16)


def mine_kernel(g, x0, x1, x2, x3, out):
    for at, piece in weight_terms(g, (x0, x1, x2, x3), lax.axis_index("c"), out.shape):
        out[at] = piece


def add_kernel(mine, got, out):
    out[...] = (mine[...] + got[...].astype(F32)).astype(BF16)


def input_kernel(g, whole, b2, *outs):
    tokens = g.shape[1]
    tile = b2.shape[0]
    grads = relative(g)
    pieces = [(at, whole[at : at + tile, :]) for at in range(0, whole.shape[0], tile)]
    pieces.append((piece_places(tile)[4], b2[...]))
    for at, w in pieces:
        term = dot(grads, w, NT).astype(BF16)
        for k, out in enumerate(outs):
            out[:, pl.ds(at, tile)] = term[k * tokens : (k + 1) * tokens]


def total_kernel(ref, out):
    out[...] = jnp.sum(ref[...].astype(F32), axis=0)


def shift(value, axis, k):
    n = lax.axis_size(axis)
    return lax.ppermute(value, axis, [(i, (i + k) % n) for i in range(n)])


def swap(value, axes):
    return lax.all_to_all(value, axes, 0, 0, tiled=True)


def z_move(value, target):
    pairs = []
    for zl in range(2):
        for zh in range(4):
            to_l, to_h = target(zl, zh)
            pairs.append((zl * 4 + zh, to_l * 4 + to_h % 4))
    return lax.ppermute(value, ("zl", "zh"), pairs)


def across(value):
    return z_move(value, lambda zl, zh: (0, zh + 1) if zl else (1, zh - 1))


def over(value):
    return z_move(value, lambda zl, zh: (zl, zh - 1 if zl else zh + 1))


def beside(value):
    return z_move(value, lambda zl, zh: (1 - zl, zh))


def on_device(inputs, segment_ids, qkv_weight, attn_cotangent):
    tokens, features = inputs.shape
    block, cols = qkv_weight.shape
    n = 4
    width = features // n
    half = block // 2
    span = cols // 32
    c = lax.axis_index("c")

    me = lax.axis_index("x")
    def cut(value, k):
        return lax.dynamic_slice_in_dim(value, lax.rem(me + k, n) * width, width, 1)

    opposite, rest = lax.optimization_barrier((cut(inputs, 2), inputs))
    own = lax.dynamic_slice_in_dim(qkv_weight, c * half, half, 0)
    a, same, ahead, behind = lax.optimization_barrier((across(own), cut(rest, 0), cut(rest, 1), cut(rest, 3)))
    sent = [same, ahead, opposite, behind]
    x2 = shift(sent[2], "x", 2)
    x2, ahead, behind = lax.optimization_barrier((x2, sent[1], sent[3]))
    x1 = shift(ahead, "x", 1)
    x3 = shift(behind, "x", 3)
    a2 = shift(a, "c", 1)
    b = beside(a)
    b2 = shift(b, "c", 1)
    d = over(a)
    d2 = shift(d, "c", 1)
    xs = (sent[0], x1, x2, x3)

    flops = 2 * n * tokens * width * cols
    whole, begun = pl.pallas_call(
        forward_kernel,
        out_shape=[arr((width, cols)), arr(((n - 1) * tokens, cols), F32)],
        compiler_params=PARAMS,
        cost_estimate=cost(flops * 3 // 4, 8 << 20),
        name="forward",
    )(*xs[:3], qkv_weight, a, a2, b, d, d2)
    parts = pl.pallas_call(
        last_forward_kernel,
        out_shape=arr((n, tokens, cols)),
        compiler_params=PARAMS,
        cost_estimate=cost(flops // 4, 5 << 20),
        name="last_forward",
    )(*xs, qkv_weight, a, a2, b, b2, d, d2, begun)
    parts = swap(parts, "x")

    grads = pl.pallas_call(
        attention_kernel,
        out_shape=arr((tokens, cols)),
        compiler_params=PARAMS,
        cost_estimate=cost(1 << 28, 1 << 20),
        name="attention",
    )(parts, segment_ids, attn_cotangent)
    grads = lax.all_gather(grads, "x", axis=0, tiled=False)

    share = arr((64, span, block))
    other = pl.pallas_call(
        other_kernel,
        out_shape=share,
        compiler_params=PARAMS,
        cost_estimate=cost(flops // 2, 4 << 20),
        name="weight_grad_other_core",
    )(grads, *xs)
    got = shift(other, "c", 1)

    back = pl.pallas_call(
        input_kernel,
        out_shape=[arr((tokens, width))] * n,
        compiler_params=PARAMS,
        cost_estimate=cost(flops, 6 << 20),
        name="input_grad",
    )(grads, whole, b2)
    got, back = lax.optimization_barrier((got, back))
    home = [back[0]] + [shift(back[k], "x", n - k) for k in range(1, n)]

    mine = pl.pallas_call(
        mine_kernel,
        out_shape=arr(share.shape, F32),
        compiler_params=PARAMS,
        cost_estimate=cost(flops // 2, 6 << 20),
        name="weight_grad_this_core",
    )(grads, *xs)
    summed = pl.pallas_call(
        add_kernel,
        out_shape=share,
        compiler_params=PARAMS,
        cost_estimate=cost(1 << 20, 6 << 20),
        name="add_cores",
    )(mine, got)
    pieces = swap(summed, ("zl", "y", "zh"))
    weight_grad = pl.pallas_call(
        total_kernel,
        out_shape=arr((span, block), F32),
        compiler_params=PARAMS,
        cost_estimate=cost(1 << 20, 2 << 20),
        name="add_replicas",
    )(pieces).T

    input_grad = pl.pallas_call(
        join_kernel,
        out_shape=arr((tokens, features)),
        compiler_params=PARAMS,
        cost_estimate=cost(1 << 20, 4 << 20),
        name="join_features",
    )(*home)
    return (input_grad, weight_grad)


def solution(mesh):
    outer, inner = ("zl", "y", "c"), ("x", "zh")
    fine = Mesh(mesh.devices.reshape(2, 8, 2, 4, 4), outer + inner)
    return jax.shard_map(
        on_device,
        mesh=fine,
        in_specs=(
            P(outer + inner, None),
            P(outer + inner, None),
            P(inner, None),
            P(outer + inner, None),
        ),
        out_specs=(P(outer + inner, None), P(inner, outer)),
        check_vma=False,
    )
```
